256 devices in a mesh: tensor: 16 (over y, x_lo, core), fsdp: 16 (over x_hi, z).
Axes of the slice: x: 4 (x_hi: 2, x_lo: 2; x = x_hi * 2 + x_lo), y: 4, z: 8, core: 2. Of those that a mesh axis runs over, the one named last changes fastest.
Arguments:
- tokens: bfloat16 [8192, 8192], P('fsdp', 'tensor'), may hold values from -6 to 6
- gate_weight: bfloat16 [8192, 4096], P('fsdp', 'tensor'), may hold values from -0.0625 to 0.0625
- up_weight: bfloat16 [8192, 4096], P('fsdp', 'tensor'), may hold values from -0.0625 to 0.0625
- hidden_grad: bfloat16 [8192, 4096], P('fsdp', 'tensor'), may hold values from -2 to 2
Outputs:
- hidden: bfloat16 [8192, 4096], P('fsdp', 'tensor')
- input_grad: bfloat16 [8192, 8192], P('fsdp', 'tensor')
- gate_grad: float32 [8192, 4096], P('fsdp', 'tensor')
- up_grad: float32 [8192, 4096], P('fsdp', 'tensor')
The draws below stay inside these ranges and needn't reach their ends.
All inputs are finite; a program needn't handle non-finite values.
Results may differ from the reference program's by a relative error of at most 0.0049.
Values may be sent and summed in bfloat16 or wider, within the bound.
A program may use at most 128 MiB of HBM per device.

```python
import jax
import jax.numpy as jnp

D = 8192
FF = 4096
TOKENS = 8192


def strengthened(entries, stream_key, source, target, parts, factor):
    def block_of(axis_at):
        return (jnp.arange(entries.shape[axis_at]) // (entries.shape[axis_at] // parts)).reshape((-1,) + (1,) * (entries.ndim - 1 - axis_at))

    first = jax.random.permutation(stream_key, parts)[block_of(target)]
    second = (block_of(target) + parts // 2) % parts
    return jnp.where((block_of(source) == first) | (block_of(source) == second), factor * entries, entries)


def block_levels(rng, dims, pieces, low, high):
    gain = 1.0
    for position, blocks in pieces:
        draws = jax.random.uniform(jax.random.fold_in(jax.random.fold_in(rng, 6), position), (blocks,), jnp.float32, low / len(pieces), high / len(pieces))
        gain = gain * jnp.repeat(jnp.exp(draws), dims[position] // blocks).reshape((-1,) + (1,) * (len(dims) - 1 - position))
    return gain


def normal_values(stream_key, shape, width, limit, cuts=(), kind=jnp.bfloat16):
    gain = block_levels(stream_key, shape, cuts, -0.22, 0.18) if cuts else 1.0
    values = jax.random.normal(stream_key, shape, jnp.float32) * width * gain
    return jnp.minimum(jnp.maximum(values, -limit), limit).astype(kind)


def heavy_noise(own_key, extent, deviation, limit, pieces, heavy, kind=jnp.bfloat16):
    entries = deviation * jax.random.normal(own_key, extent, jnp.float32)
    if pieces:
        entries = entries * block_levels(own_key, extent, pieces, -0.22, 0.18)
    return jnp.clip(strengthened(entries, jax.random.fold_in(own_key, 3), *heavy), -limit, limit).astype(kind)


def setup_inputs(seed: int = 0) -> dict:
    key_of = jax.random.split(jax.random.key(seed), 5)
    return {
        "tokens": heavy_noise(key_of[0], (TOKENS, D), 1.0, 6.0, ((0, 16), (1, 16)), (0, 1, 16, 2.0)),
        "gate_weight": normal_values(key_of[1], (D, FF), D ** -0.5, 0.0625, ((0, 16), (1, 16))),
        "up_weight": normal_values(key_of[2], (D, FF), D ** -0.5, 0.0625, ((0, 16), (1, 16))),
        "hidden_grad": normal_values(key_of[3], (TOKENS, FF), 0.15, 2.0, ((0, 16), (1, 16))),
    }


def reference(tokens, gate_weight, up_weight, hidden_grad):
    gate = jnp.dot(tokens, gate_weight, preferred_element_type=jnp.float32)
    up = jnp.dot(tokens, up_weight, preferred_element_type=jnp.float32)
    sig = jax.nn.sigmoid(gate)
    active = gate * sig
    hidden = (active * up).astype(jnp.bfloat16)
    upstream = hidden_grad.astype(jnp.float32)
    dgate = (upstream * up * sig * (1.0 + gate * (1.0 - sig))).astype(jnp.bfloat16)
    dup = (upstream * active).astype(jnp.bfloat16)
    input_grad = (jnp.dot(dgate, gate_weight.T, preferred_element_type=jnp.float32)
                  + jnp.dot(dup, up_weight.T, preferred_element_type=jnp.float32)).astype(jnp.bfloat16)
    gate_grad = jnp.dot(tokens.T, dgate, preferred_element_type=jnp.float32)
    up_grad = jnp.dot(tokens.T, dup, preferred_element_type=jnp.float32)
    return hidden, input_grad, gate_grad, up_grad
```

```python
import functools

import jax
import jax.numpy as jnp
from jax import lax
from jax.experimental import pallas as pl
from jax.experimental.pallas import tpu as pltpu
from jax.sharding import PartitionSpec as P

MESH = pl.DeviceIdType.MESH
F32 = jnp.float32
BF16 = jnp.bfloat16
B = 512
H = 256
HALF = (slice(0, H), slice(H, B))
N_SEMS = 80


def kernel(tok, gw, uw, hg, hidden_o, ig_o, gg_o, ug_o,
           t_all, w_all, acc, crecv, dg, igk, igs, igr, y1s, y1r, y2s, y2r, ls, lr, sws, swr, wgb, zs, zr,
           send_sem, recv_sem):
    f = lax.axis_index("fsdp")
    t = lax.axis_index("tensor")
    h, z = f // 8, f % 8
    y, l, c = t // 4, (t // 2) % 2, t % 2
    odd = (y // 2 + h) % 2

    def dev(hh=h, zz=z, yy=y, ll=l, cc=c):
        return {"tensor": (yy % 4) * 4 + ll * 2 + cc, "fsdp": hh * 8 + zz % 8}

    right, left = dev(zz=z + 1), dev(zz=z + 7)
    sib, lnb = dev(cc=1 - c), dev(ll=1 - l)
    yr, yl = dev(yy=y + 1), dev(yy=y + 3)
    swap, hpeer = dev(hh=1 - h, yy=3 - y), dev(hh=1 - h)

    barrier = pltpu.get_barrier_semaphore()
    for d in (right, left, sib, lnb, yr, yl, swap, hpeer):
        pl.semaphore_signal(barrier, inc=1, device_id=d, device_id_type=MESH)
    pl.semaphore_wait(barrier, 8)

    n_used = [0]
    sends = []

    class Copy:
        def __init__(self, src, dst, device, arrives=None):
            k = n_used[0]
            n_used[0] += 1
            assert k < N_SEMS
            make = lambda a, b: pltpu.make_async_remote_copy(
                src_ref=a, dst_ref=b, send_sem=send_sem.at[k], recv_sem=recv_sem.at[k],
                device_id=device, device_id_type=MESH)
            self.out = make(src, dst)
            self.into = make(src, dst if arrives is None else arrives)

        def start(self):
            self.out.start()
            sends.append(self.out)
            return self

        def arrived(self):
            self.into.wait_recv()

    w_all[z, :, :H] = gw[...]
    w_all[z, :, H:] = uw[...]

    def w_copy(way, s, half):
        out, into = ((z + 8 - s) % 8, (z + 7 - s) % 8) if way == 0 else ((z + s) % 8, (z + 1 + s) % 8)
        rows = pl.ds(half * H, H)
        return Copy(w_all.at[out, rows], w_all.at[out, rows], right if way == 0 else left, w_all.at[into, rows])

    w = {}
    for s in range(4):
        for half in range(2):
            for way in range(2):
                if s < 3 or half == way:
                    w[way, s, half] = w_copy(way, s, half)

    def w_start(s, first):
        for k in ((0, 1) if s < 3 else (0,)):
            for way in range(2):
                half = way if k == 0 else 1 - way
                if not first:
                    w[way, s - 1, half].arrived()
                w[way, s, half].start()

    w_start(0, True)

    mine, at_l = t_all.at[t], t_all.at[y * 4 + (1 - l) * 2 + c]
    t_peer = (3 - y) * 4 + l * 2 + c
    swp = Copy(tok, t_all.at[t_peer], swap, mine)

    @pl.when(odd == 1)
    def _():
        swp.out.start()

    @pl.when(odd == 0)
    def _():
        t_all[t] = tok[...]

    @pl.when(odd == 1)
    def _():
        swp.into.wait_recv()

    def slot(yy, ll, cc):
        return (yy % 4) * 4 + ll * 2 + cc

    def to_sib(yy, ll, rows=slice(None)):
        a, b = slot(yy, ll, c), slot(yy, ll, 1 - c)
        r = pl.ds(0, B) if rows == slice(None) else rows
        return Copy(t_all.at[a, r], t_all.at[a, r], sib, t_all.at[b, r]).start()

    def along_y(way, yy, ll, rows):
        src = slot(yy, ll, c)
        into = slot(yy + (3 if way == 0 else 1), ll, c)
        return Copy(t_all.at[src, rows], t_all.at[src, rows], yr if way == 0 else yl, t_all.at[into, rows]).start()

    full, ra, rb = pl.ds(0, B), pl.ds(0, H), pl.ds(H, H)
    from_sib = []
    by_l = Copy(mine, mine, lnb, at_l).start()
    y_own = [along_y(way, y, l, full) for way in range(2)]
    from_sib.append(to_sib(y, l))
    w_start(1, False)
    by_l.arrived()
    y_nbr = [along_y(way, y, 1 - l, full) for way in range(2)]
    from_sib.append(to_sib(y, 1 - l))
    far = []
    for way in range(2):
        y_own[way].arrived()
        yy = y + (3 if way == 0 else 1)
        far.append((way, l, along_y(way, yy, l, ra if way == 0 else rb)))
        from_sib.append(to_sib(yy, l))
    w_start(2, False)
    for way in range(2):
        y_nbr[way].arrived()
        yy = y + (3 if way == 0 else 1)
        far.append((way, 1 - l, along_y(way, yy, 1 - l, ra if way == 0 else rb)))
        from_sib.append(to_sib(yy, 1 - l))
    w_start(3, False)
    for way, ll, copy in far:
        copy.arrived()
        from_sib.append(to_sib(y + 2, ll, ra if way == 0 else rb))
    w[0, 3, 0].arrived()
    w[1, 3, 1].arrived()
    w[0, 2, 1].arrived()
    w[1, 2, 0].arrived()
    for copy in from_sib:
        copy.arrived()

    def place(yy, ll, cc):
        rr = (yy // 2 + h) % 2
        return rr, ((yy + rr) % 2) * 4 + ll * 2 + cc

    def fwd(p, _):
        rr, kb = place(p // 4, (p // 2) % 2, p % 2)
        for n in range(2):
            cols = pl.ds(n * H, H)
            acc[rr, :, cols] += jnp.dot(t_all[p], w_all[kb, :, cols], preferred_element_type=F32)
        return 0

    acc[...] = jnp.zeros_like(acc)
    lax.fori_loop(0, 16, fwd, 0)
    c_part = Copy(acc.at[1], crecv, hpeer).start()
    c_part.arrived()

    def gated(i, _):
        rows = pl.ds(i * 64, 64)
        gate = acc[0, rows, :H] + crecv[rows, :H]
        up = acc[0, rows, H:] + crecv[rows, H:]
        sig = jax.nn.sigmoid(gate)
        active = gate * sig
        upstream = hg[rows].astype(F32)
        hidden_o[rows] = (active * up).astype(BF16)
        dg[0, rows, :H] = (upstream * up * sig * (1.0 + gate * (1.0 - sig))).astype(BF16)
        dg[0, rows, H:] = (upstream * active).astype(BF16)
        return 0

    lax.fori_loop(0, 8, gated, 0)
    d_part = Copy(dg.at[0], dg.at[1], hpeer).start()
    d_part.arrived()

    def ig_block(yy, ll, cc, store):
        rr, kb = place(yy, ll, cc)
        for n in range(2):
            cols = pl.ds(n * H, H)
            store(cols, lax.dot_general(dg[rr], w_all[kb, cols, :], (((1,), (1,)), ((), ())),
                                        preferred_element_type=F32))

    def ig_for_sib(yy):
        yy = yy % 4

        def one(ll, _):
            def store(cols, v):
                igs[yy * 2 + ll, :, cols] = v.astype(BF16)
            ig_block(yy, ll, 1 - c, store)
            return 0
        lax.fori_loop(0, 2, one, 0)
        two = pl.ds(yy * 2, 2)
        return Copy(igs.at[two], igr.at[two], sib).start()

    def ig_own(yy):
        yy = yy % 4

        def one(ll, _):
            def store(cols, v):
                igk[yy * 2 + ll, :, cols] = v
            ig_block(yy, ll, c, store)
            return 0
        lax.fori_loop(0, 2, one, 0)

    def wg_block(j, buf):
        j = j % 8

        for n in range(2):
            ks = pl.ds(n * H, H)
            total = None
            for rr in range(2):
                yy = 2 * ((h + rr) % 2) + (j // 4 + rr) % 2
                v = lax.dot_general(t_all[yy * 4 + j % 4, :, ks], dg[rr], (((0,), (0,)), ((), ())),
                                    preferred_element_type=F32)
                total = v if total is None else total + v
            wgb[buf, ks, :] = total

    def rowwise(start, size, body):
        def one(i, _):
            body(pl.ds(start + i * 64, 64))
            return 0
        lax.fori_loop(0, size // 64, one, 0)

    zc = {}

    def z_send(way, s, half):
        rows = pl.ds(half * H, H)
        zc[way, s, half] = Copy(zs.at[way, s, rows], zr.at[way, s, rows], right if way == 0 else left).start()

    def z_step(way, s, half, buf):
        add = s >= 1 if half == way else s >= 2
        if add:
            zc[way, s - 1, half].arrived()

        def body(rows):
            v = wgb[buf, rows]
            if add:
                v = v + zr[way, s - 1, rows].astype(F32)
            zs[way, s, rows] = v.astype(BF16)
        rowwise(half * H, H, body)
        z_send(way, s, half)

    wg_block(z + 4, 0)
    z_step(0, 0, 0, 0)
    z_step(1, 0, 1, 0)
    sib2 = ig_for_sib(y + 2)
    wg_block(z + 3, 0)
    wg_block(z + 5, 1)
    z_step(0, 1, 1, 0)
    z_step(1, 1, 0, 1)
    ig_own(y + 2)
    sib_near = [ig_for_sib(y + 1), ig_for_sib(y + 3)]
    z_step(0, 1, 0, 0)
    z_step(1, 1, 1, 1)
    sib2.arrived()
    op = ((y + 2) % 4) * 2
    y1 = []
    for way, half in ((0, 0), (1, 1)):
        for ll in range(2):
            def body(rows):
                y1s[ll, rows] = (igk[op + ll, rows] + igr[op + ll, rows].astype(F32)).astype(BF16)
            rowwise(half * H, H, body)
        rows = pl.ds(half * H, H)
        y1.append(Copy(y1s.at[:, rows], y1r.at[:, rows], yr if way == 0 else yl).start())
    ig_own(y + 1)
    ig_own(y + 3)
    y2 = []

    def y_stage(way, half, add):
        near = ((y + (1 if way == 0 else 3)) % 4) * 2
        for ll in range(2):
            def body(rows):
                v = igk[near + ll, rows] + igr[near + ll, rows].astype(F32)
                if add:
                    v = v + y1r[ll, rows].astype(F32)
                y2s[way, ll, rows] = v.astype(BF16)
            rowwise(half * H, H, body)
        rows = pl.ds(half * H, H)
        y2.append((way, Copy(y2s.at[way, :, rows], y2r.at[way, :, rows], yr if way == 0 else yl).start()))

    for way in range(2):
        sib_near[way].arrived()
        y_stage(way, 1 - way, False)
    wg_block(z + 2, 0)
    wg_block(z + 6, 1)
    z_step(0, 2, 1, 0)
    z_step(1, 2, 0, 1)
    z_step(0, 2, 0, 0)
    z_step(1, 2, 1, 1)
    y1[0].arrived()
    y_stage(0, 0, True)
    y1[1].arrived()
    y_stage(1, 1, True)
    sib_own = ig_for_sib(y)
    ig_own(y)
    wg_block(z + 1, 0)
    wg_block(z + 7, 1)
    z_step(0, 3, 1, 0)
    z_step(1, 3, 0, 1)
    z_step(0, 3, 0, 0)
    z_step(1, 3, 1, 1)
    wg_block(z, 0)
    sib_own.arrived()
    for _, copy in y2:
        copy.arrived()

    def y_total(ll, rows):
        v = igk[y * 2 + ll, rows] + igr[y * 2 + ll, rows].astype(F32)
        return v + y2r[0, ll, rows].astype(F32) + y2r[1, ll, rows].astype(F32)

    def body(rows):
        ls[rows] = y_total(1 - l, rows).astype(BF16)
    rowwise(0, B, body)
    l_part = Copy(ls, lr, lnb).start()
    l_part.arrived()

    def body(rows):
        sws[rows] = (y_total(l, rows) + lr[rows].astype(F32)).astype(BF16)
    rowwise(0, B, body)
    back = Copy(sws, swr, swap)

    @pl.when(odd == 1)
    def _():
        back.out.start()

    for half in range(2):
        zc[0, 3, half].arrived()
        zc[1, 3, half].arrived()

    def body(rows):
        v = wgb[0, rows] + zr[0, 3, rows].astype(F32) + zr[1, 3, rows].astype(F32)
        gg_o[rows] = v[:, :H]
        ug_o[rows] = v[:, H:]
    rowwise(0, B, body)

    @pl.when(odd == 0)
    def _():
        ig_o[...] = sws[...]

    @pl.when(odd == 1)
    def _():
        back.into.wait_recv()
        ig_o[...] = swr[...]
        swp.out.wait_send()
        back.out.wait_send()

    for copy in sends:
        copy.wait_send()


def body(tokens, gate_weight, up_weight, hidden_grad):
    vm = pl.BlockSpec(memory_space=pltpu.VMEM)
    return pl.pallas_call(
        kernel,
        out_shape=(
            jax.ShapeDtypeStruct((B, H), BF16),
            jax.ShapeDtypeStruct((B, B), BF16),
            jax.ShapeDtypeStruct((B, H), F32),
            jax.ShapeDtypeStruct((B, H), F32),
        ),
        in_specs=[vm] * 4,
        out_specs=(vm,) * 4,
        scratch_shapes=[
            pltpu.VMEM((16, B, B), BF16),
            pltpu.VMEM((8, B, B), BF16),
            pltpu.VMEM((2, B, B), F32),
            pltpu.VMEM((B, B), F32),
            pltpu.VMEM((2, B, B), BF16),
            pltpu.VMEM((8, B, B), F32),
            pltpu.VMEM((8, B, B), BF16),
            pltpu.VMEM((8, B, B), BF16),
            pltpu.VMEM((2, B, B), BF16),
            pltpu.VMEM((2, B, B), BF16),
            pltpu.VMEM((2, 2, B, B), BF16),
            pltpu.VMEM((2, 2, B, B), BF16),
            pltpu.VMEM((B, B), BF16),
            pltpu.VMEM((B, B), BF16),
            pltpu.VMEM((B, B), BF16),
            pltpu.VMEM((B, B), BF16),
            pltpu.VMEM((2, B, B), F32),
            pltpu.VMEM((2, 4, B, B), BF16),
            pltpu.VMEM((2, 4, B, B), BF16),
            pltpu.SemaphoreType.DMA((N_SEMS,)),
            pltpu.SemaphoreType.DMA((N_SEMS,)),
        ],
        compiler_params=pltpu.CompilerParams(
            collective_id=0, has_side_effects=True, vmem_limit_bytes=60 * 1024 * 1024
        ),
    )(tokens, gate_weight, up_weight, hidden_grad)


def solution(mesh):
    spec = P("fsdp", "tensor")
    return jax.shard_map(body, mesh=mesh, in_specs=(spec,) * 4, out_specs=(spec,) * 4, check_vma=False)
```

```python
import functools

import jax
import jax.numpy as jnp
from jax import lax
from jax.experimental import pallas as pl
from jax.experimental.pallas import tpu as pltpu
from jax.sharding import PartitionSpec as P

MESH = pl.DeviceIdType.MESH
F32 = jnp.float32
BF16 = jnp.bfloat16
B = 512
H = 256
Q = 128
N_SEMS = 128


def kernel(tok, gw, uw, hg, hidden_o, ig_o, gg_o, ug_o,
           t_all, w_all, acc, cs, cr, dg, igk, igs, igr, ds, dr, es, er, ls, lr, sws, swr, wgb, zs, zr,
           send_sem, recv_sem):
    f = lax.axis_index("fsdp")
    t = lax.axis_index("tensor")
    h, z = f // 8, f % 8
    y, l, c = t // 4, (t // 2) % 2, t % 2
    odd = (y // 2 + h) % 2

    def dev(hh=h, zz=z, yy=y, ll=l, cc=c):
        return {"tensor": (yy % 4) * 4 + ll * 2 + cc, "fsdp": hh * 8 + zz % 8}

    right, left = dev(zz=z + 1), dev(zz=z + 7)
    sib, lnb = dev(cc=1 - c), dev(ll=1 - l)
    yr, yl = dev(yy=y + 1), dev(yy=y + 3)
    swap, hpeer = dev(hh=1 - h, yy=3 - y), dev(hh=1 - h)

    barrier = pltpu.get_barrier_semaphore()
    for d in (right, left, sib, lnb, yr, yl, swap, hpeer):
        pl.semaphore_signal(barrier, inc=1, device_id=d, device_id_type=MESH)
    pl.semaphore_wait(barrier, 8)

    n_used = [0]
    sends = []

    class Copy:
        def __init__(self, src, dst, device, arrives=None):
            self.k = n_used[0]
            n_used[0] += 1
            assert self.k < N_SEMS
            self.src, self.dst, self.device = src, dst, device
            self.into = dst if arrives is None else arrives

        def make(self, src, dst):
            return pltpu.make_async_remote_copy(
                src_ref=src, dst_ref=dst, send_sem=send_sem.at[self.k], recv_sem=recv_sem.at[self.k],
                device_id=self.device, device_id_type=MESH)

        def start(self, listed=True):
            self.make(self.src, self.dst).start()
            if listed and self not in sends:
                sends.append(self)
            return self

        def arrived(self):
            self.make(self.src, self.into).wait_recv()

        def sent(self):
            self.make(self.src, self.dst).wait_send()

    def rowwise(start, size, body):
        def one(i, _):
            body(pl.ds(start + i * 64, 64))
            return 0
        lax.fori_loop(0, size // 64, one, 0)

    for n in range(2):
        part = slice(n * Q, (n + 1) * Q)
        w_all[z, :, n * H:n * H + Q] = gw[:, part]
        w_all[z, :, n * H + Q:(n + 1) * H] = uw[:, part]

    def w_copy(way, s, half):
        out, into = ((z + 8 - s) % 8, (z + 7 - s) % 8) if way == 0 else ((z + s) % 8, (z + 1 + s) % 8)
        rows = pl.ds(half * H, H)
        return Copy(w_all.at[out, rows], w_all.at[out, rows], right if way == 0 else left, w_all.at[into, rows])

    w = {}
    for s in range(4):
        for half in range(2):
            for way in range(2):
                if s < 3 or half == way:
                    w[way, s, half] = w_copy(way, s, half)

    def w_start(s, first):
        for k in ((0, 1) if s < 3 else (0,)):
            for way in range(2):
                half = way if k == 0 else 1 - way
                if not first:
                    w[way, s - 1, half].arrived()
                w[way, s, half].start()

    w_start(0, True)

    mine, at_l = t_all.at[t], t_all.at[y * 4 + (1 - l) * 2 + c]
    t_peer = (3 - y) * 4 + l * 2 + c
    swp = Copy(tok, t_all.at[t_peer], swap, mine)

    @pl.when(odd == 1)
    def _():
        swp.start(False)

    @pl.when(odd == 0)
    def _():
        t_all[t] = tok[...]

    @pl.when(odd == 1)
    def _():
        swp.arrived()

    def slot(yy, ll, cc):
        return (yy % 4) * 4 + ll * 2 + cc

    def to_sib(yy, ll, rows=slice(None)):
        a, b = slot(yy, ll, c), slot(yy, ll, 1 - c)
        r = pl.ds(0, B) if rows == slice(None) else rows
        return Copy(t_all.at[a, r], t_all.at[a, r], sib, t_all.at[b, r]).start()

    def along_y(way, yy, ll, rows):
        src = slot(yy, ll, c)
        into = slot(yy + (3 if way == 0 else 1), ll, c)
        return Copy(t_all.at[src, rows], t_all.at[src, rows], yr if way == 0 else yl, t_all.at[into, rows]).start()

    full, ra, rb = pl.ds(0, B), pl.ds(0, H), pl.ds(H, H)
    from_sib = []
    by_l = Copy(mine, mine, lnb, at_l).start()
    y_own = [along_y(way, y, l, full) for way in range(2)]
    from_sib.append(to_sib(y, l))
    w_start(1, False)
    by_l.arrived()
    y_nbr = [along_y(way, y, 1 - l, full) for way in range(2)]
    from_sib.append(to_sib(y, 1 - l))
    far = []
    for way in range(2):
        y_own[way].arrived()
        yy = y + (3 if way == 0 else 1)
        far.append((way, l, along_y(way, yy, l, ra if way == 0 else rb)))
        from_sib.append(to_sib(yy, l))
    w_start(2, False)
    for way in range(2):
        y_nbr[way].arrived()
        yy = y + (3 if way == 0 else 1)
        far.append((way, 1 - l, along_y(way, yy, 1 - l, ra if way == 0 else rb)))
        from_sib.append(to_sib(yy, 1 - l))
    w_start(3, False)
    w[0, 3, 0].arrived()
    w[1, 3, 1].arrived()
    w[0, 2, 1].arrived()
    w[1, 2, 0].arrived()
    for copy in from_sib:
        copy.arrived()

    def place(yy, ll, cc):
        rr = (yy // 2 + h) % 2
        return rr, ((yy + rr) % 2) * 4 + ll * 2 + cc

    def fwd(yy, parts):
        yy = yy % 4

        def one(i, _):
            rr, kb = place(yy, i // 2, i % 2)
            for n in parts:
                acc[n, rr] += jnp.dot(t_all[yy * 4 + i], w_all[kb, :, n * H:(n + 1) * H], preferred_element_type=F32)
            return 0
        lax.fori_loop(0, 4, one, 0)

    acc[...] = jnp.zeros_like(acc)
    for off in (0, 1, 3):
        fwd(y + off, (0, 1))
    late = []
    for way, ll, copy in far:
        copy.arrived()
        late.append(to_sib(y + 2, ll, ra if way == 0 else rb))
    for copy in late:
        copy.arrived()

    c_part, d_part = [], []
    for n in range(2):
        fwd(y + 2, (n,))

        def body(rows):
            cs[n, rows] = acc[n, 1, rows].astype(cs.dtype)
        rowwise(0, B, body)
        c_part.append(Copy(cs.at[n], cr.at[n], hpeer).start())

    for n in range(2):
        c_part[n].arrived()

        def body(rows):
            v = acc[n, 0, rows] + cr[n, rows].astype(F32)
            gate, up = v[:, :Q], v[:, Q:]
            sig = jax.nn.sigmoid(gate)
            active = gate * sig
            part = slice(n * Q, (n + 1) * Q)
            upstream = hg[rows, part].astype(F32)
            hidden_o[rows, part] = (active * up).astype(BF16)
            dg[n, 0, rows, :Q] = (upstream * up * sig * (1.0 + gate * (1.0 - sig))).astype(BF16)
            dg[n, 0, rows, Q:] = (upstream * active).astype(BF16)
        rowwise(0, B, body)
        d_part.append(Copy(dg.at[n, 0], dg.at[n, 1], hpeer).start())

    sign = 1 - 2 * (y % 2)
    y0, y1 = y + sign, (y - sign + 4) % 4
    d0, d1 = dev(yy=y0), dev(yy=y1)

    def ig_set(r, k):
        target = (odd + r + 1) % 2
        yy = (target * y0 + (1 - target) * ((y + 2) % 4)) if k == 0 else (target * y + (1 - target) * y1)

        def block(ll, cc, store):
            _, kb = place(yy, ll, cc)
            for half in range(2):
                ks = pl.ds(half * H, H)
                total = None
                for n in range(2):
                    v = lax.dot_general(dg[n, r], w_all[kb, ks, n * H:(n + 1) * H], (((1,), (1,)), ((), ())),
                                        preferred_element_type=F32)
                    total = v if total is None else total + v
                store(ll, ks, total)

        def to_other(ll, ks, v):
            igs[r, k, ll, :, ks] = v.astype(BF16)

        def to_own(ll, ks, v):
            igk[r, k, ll, :, ks] = v

        def one(ll, _):
            block(ll, 1 - c, to_other)
            return 0
        lax.fori_loop(0, 2, one, 0)
        copy = Copy(igs.at[r, k], igr.at[r, k], sib).start()

        def one(ll, _):
            block(ll, c, to_own)
            return 0
        lax.fori_loop(0, 2, one, 0)
        return copy

    def both(i, ll, rows, r):
        return igk[r, i, ll, rows] + igr[r, i, ll, rows].astype(F32)

    rows_of = [pl.ds(k * Q, Q) for k in range(4)]
    to_d0 = {(r, k): Copy(ds.at[r, :, rows_of[k]], dr.at[r, :, rows_of[k]], d0) for r in range(2) for k in range(4)}
    to_d1 = [Copy(es.at[:, rows_of[k]], er.at[:, rows_of[k]], d1) for k in range(4)]
    to_l = [Copy(ls.at[rows_of[k]], lr.at[rows_of[k]], lnb) for k in range(4)]
    back = [Copy(sws.at[rows_of[k]], swr.at[rows_of[k]], swap) for k in range(4)]

    def send_d0(r, *parts):
        for k in parts:
            for ll in range(2):
                def body(rows):
                    ds[r, ll, rows] = both(0, ll, rows, r).astype(BF16)
                rowwise(k * Q, Q, body)
            to_d0[r, k].start()

    def send_d1(r, *parts):
        for k in parts:
            to_d0[r, k].arrived()
            for ll in range(2):
                def body(rows):
                    es[ll, rows] = (both(1, ll, rows, r) + dr[r, ll, rows].astype(F32)).astype(BF16)
                rowwise(k * Q, Q, body)
            to_d1[k].start()

    def total(r, ll, rows):
        return both(1, ll, rows, r) + dr[r, ll, rows].astype(F32) + er[ll, rows].astype(F32)

    def send_l(r, *parts):
        for k in parts:
            to_d0[r, k].arrived()
            to_d1[k].arrived()

            def body(rows):
                ls[rows] = total(r, 1 - l, rows).astype(BF16)
            rowwise(k * Q, Q, body)
            to_l[k].start()

    def finish(r, *parts):
        for k in parts:
            to_l[k].arrived()

            def body(rows):
                v = (total(r, l, rows) + lr[rows].astype(F32)).astype(BF16)
                if r == 0:
                    ig_o[rows] = v
                else:
                    sws[rows] = v
            rowwise(k * Q, Q, body)
            if r == 1:
                back[k].start(False)

    def when(is_odd, body, *args):
        @pl.when(odd == is_odd)
        def _():
            body(*args)

    def wg_block(j, buf, n):
        j = j % 8
        for half in range(2):
            ks = pl.ds(half * H, H)
            v = None
            for rr in range(2):
                yy = 2 * ((h + rr) % 2) + (j // 4 + rr) % 2
                u = lax.dot_general(t_all[yy * 4 + j % 4, :, ks], dg[n, rr], (((0,), (0,)), ((), ())),
                                    preferred_element_type=F32)
                v = u if v is None else v + u
            wgb[buf, n, ks, :] = v

    zc = {}

    def z_step(way, s, half, n):
        add = s >= 1 if half == way else s >= 2
        if add:
            zc[way, s - 1, half, n].arrived()

        def body(rows):
            v = wgb[way, n, rows]
            if add:
                v = v + zr[way, s - 1, n, rows].astype(F32)
            zs[way, s, n, rows] = v.astype(BF16)
        rowwise(half * H, H, body)
        rows = pl.ds(half * H, H)
        zc[way, s, half, n] = Copy(zs.at[way, s, n, rows], zr.at[way, s, n, rows], right if way == 0 else left).start()

    def z_begin(n):
        wg_block(z + 4, 0, n)

        def body(rows):
            wgb[1, n, rows] = wgb[0, n, rows]
        rowwise(H, H, body)
        z_step(0, 0, 0, n)
        z_step(1, 0, 1, n)
        z_blocks(1, n)
        z_step(0, 1, 1, n)
        z_step(1, 1, 0, n)

    def z_blocks(s, n):
        wg_block(z + 4 - s, 0, n)
        wg_block(z + 4 + s, 1, n)

    def z_first(n):
        z_step(0, 1, 0, n)
        z_step(1, 1, 1, n)

    def z_next(s, n):
        z_blocks(s, n)
        z_step(0, s, 1, n)
        z_step(1, s, 0, n)
        z_step(0, s, 0, n)
        z_step(1, s, 1, n)

    a0 = ig_set(0, 0)
    d_part[0].arrived()
    z_begin(0)
    a0.arrived()
    send_d0(0, 0, 1)
    when(1, send_d0, 0, 2, 3)
    b0 = ig_set(0, 1)
    d_part[1].arrived()
    a1 = ig_set(1, 0)
    a1.arrived()
    send_d0(1, 0, 1, 2, 3)
    when(0, send_d0, 0, 2, 3)
    z_begin(1)
    z_first(0)
    b0.arrived()
    when(1, send_d1, 0, 0, 1)
    b1 = ig_set(1, 1)
    z_first(1)
    when(1, send_d1, 0, 2, 3)
    z_next(2, 0)
    b1.arrived()
    when(0, send_d1, 1, 0)
    z_next(2, 1)

    def e_1():
        send_l(0, 0)
        send_d1(1, 1)

    def e_2():
        send_l(0, 1)
        send_d1(1, 2)

    def o_2():
        send_l(1, 1)
        finish(1, 0)

    def o_3():
        send_l(1, 2)
        finish(1, 1)

    def e_4():
        finish(0, 0, 1)
        send_l(0, 2, 3)
        finish(0, 2, 3)

    def o_4():
        send_l(1, 3)
        finish(1, 2, 3)

    when(0, e_1)
    when(1, send_l, 1, 0)
    z_next(3, 0)
    when(0, e_2)
    when(1, o_2)
    z_next(3, 1)
    when(0, send_d1, 1, 3)
    when(1, o_3)
    for n in range(2):
        wg_block(z, 0, n)
    when(0, e_4)
    when(1, o_4)
    for n in range(2):
        for half in range(2):
            zc[0, 3, half, n].arrived()
            zc[1, 3, half, n].arrived()

        def body(rows):
            v = wgb[0, n, rows] + zr[0, 3, n, rows].astype(F32) + zr[1, 3, n, rows].astype(F32)
            part = slice(n * Q, (n + 1) * Q)
            gg_o[rows, part] = v[:, :Q]
            ug_o[rows, part] = v[:, Q:]
        rowwise(0, B, body)

    @pl.when(odd == 1)
    def _():
        for k in range(4):
            back[k].arrived()
            ig_o[k * Q:(k + 1) * Q] = swr[k * Q:(k + 1) * Q]
            back[k].sent()
        swp.sent()

    for copy in sends:
        copy.sent()


def body(tokens, gate_weight, up_weight, hidden_grad):
    vm = pl.BlockSpec(memory_space=pltpu.VMEM)
    return pl.pallas_call(
        kernel,
        out_shape=(
            jax.ShapeDtypeStruct((B, H), BF16),
            jax.ShapeDtypeStruct((B, B), BF16),
            jax.ShapeDtypeStruct((B, H), F32),
            jax.ShapeDtypeStruct((B, H), F32),
        ),
        in_specs=[vm] * 4,
        out_specs=(vm,) * 4,
        scratch_shapes=[
            pltpu.VMEM((16, B, B), BF16),
            pltpu.VMEM((8, B, B), BF16),
            pltpu.VMEM((2, 2, B, H), F32),
            pltpu.VMEM((2, B, H), BF16),
            pltpu.VMEM((2, B, H), BF16),
            pltpu.VMEM((2, 2, B, H), BF16),
            pltpu.VMEM((2, 2, 2, B, B), F32),
            pltpu.VMEM((2, 2, 2, B, B), BF16),
            pltpu.VMEM((2, 2, 2, B, B), BF16),
            pltpu.VMEM((2, 2, B, B), BF16),
            pltpu.VMEM((2, 2, B, B), BF16),
            pltpu.VMEM((2, B, B), BF16),
            pltpu.VMEM((2, B, B), BF16),
            pltpu.VMEM((B, B), BF16),
            pltpu.VMEM((B, B), BF16),
            pltpu.VMEM((B, B), BF16),
            pltpu.VMEM((B, B), BF16),
            pltpu.VMEM((2, 2, B, H), F32),
            pltpu.VMEM((2, 4, 2, B, H), BF16),
            pltpu.VMEM((2, 4, 2, B, H), BF16),
            pltpu.SemaphoreType.DMA((N_SEMS,)),
            pltpu.SemaphoreType.DMA((N_SEMS,)),
        ],
        compiler_params=pltpu.CompilerParams(
            collective_id=0, has_side_effects=True, vmem_limit_bytes=60 * 1024 * 1024
        ),
    )(tokens, gate_weight, up_weight, hidden_grad)


def solution(mesh):
    spec = P("fsdp", "tensor")
    return jax.shard_map(body, mesh=mesh, in_specs=(spec,) * 4, out_specs=(spec,) * 4, check_vma=False)
```

```python
import functools

import jax
import jax.numpy as jnp
from jax import lax
from jax.experimental import pallas as pl
from jax.experimental.pallas import tpu as pltpu
from jax.sharding import PartitionSpec as P

MESH = pl.DeviceIdType.MESH
F32 = jnp.float32
BF16 = jnp.bfloat16
B = 512
H = 256
Q = 128
N_SEMS = 128


def kernel(tok, gw, uw, hg, hidden_o, ig_o, gg_o, ug_o,
           t_all, w_all, acc, cs, cr, dg, igk, igs, igr, ds, dr, fr, es, er, ls, lr, sws, swr, wgb, zs, zr,
           send_sem, recv_sem):
    f = lax.axis_index("fsdp")
    t = lax.axis_index("tensor")
    h, z = f // 8, f % 8
    y, l, c = t // 4, (t // 2) % 2, t % 2
    odd = (y // 2 + h) % 2

    def dev(hh=h, zz=z, yy=y, ll=l, cc=c):
        return {"tensor": (yy % 4) * 4 + ll * 2 + cc, "fsdp": hh * 8 + zz % 8}

    right, left = dev(zz=z + 1), dev(zz=z + 7)
    sib, lnb = dev(cc=1 - c), dev(ll=1 - l)
    yr, yl = dev(yy=y + 1), dev(yy=y + 3)
    swap, hpeer = dev(hh=1 - h, yy=3 - y), dev(hh=1 - h)

    barrier = pltpu.get_barrier_semaphore()
    for d in (right, left, sib, lnb, yr, yl, swap, hpeer):
        pl.semaphore_signal(barrier, inc=1, device_id=d, device_id_type=MESH)
    pl.semaphore_wait(barrier, 8)

    n_used = [0]
    sends = []

    class Copy:
        def __init__(self, src, dst, device, arrives=None):
            self.k = n_used[0]
            n_used[0] += 1
            assert self.k < N_SEMS
            self.src, self.dst, self.device = src, dst, device
            self.into = dst if arrives is None else arrives

        def make(self, src, dst):
            return pltpu.make_async_remote_copy(
                src_ref=src, dst_ref=dst, send_sem=send_sem.at[self.k], recv_sem=recv_sem.at[self.k],
                device_id=self.device, device_id_type=MESH)

        def start(self, listed=True):
            self.make(self.src, self.dst).start()
            if listed and self not in sends:
                sends.append(self)
            return self

        def arrived(self):
            self.make(self.src, self.into).wait_recv()

        def sent(self):
            self.make(self.src, self.dst).wait_send()

    def rowwise(start, size, body):
        def one(i, _):
            body(pl.ds(start + i * 64, 64))
            return 0
        lax.fori_loop(0, size // 64, one, 0)

    for n in range(2):
        part = slice(n * Q, (n + 1) * Q)
        w_all[z, :, n * H:n * H + Q] = gw[:, part]
        w_all[z, :, n * H + Q:(n + 1) * H] = uw[:, part]

    def w_copy(way, s, half):
        out, into = ((z + 8 - s) % 8, (z + 7 - s) % 8) if way == 0 else ((z + s) % 8, (z + 1 + s) % 8)
        rows = pl.ds(half * H, H)
        return Copy(w_all.at[out, rows], w_all.at[out, rows], right if way == 0 else left, w_all.at[into, rows])

    w = {}
    for s in range(4):
        for half in range(2):
            for way in range(2):
                if s < 3 or half == way:
                    w[way, s, half] = w_copy(way, s, half)

    def w_start(s, k):
        for way in range(2):
            half = way if k == 0 else 1 - way
            if s > 0:
                w[way, s - 1, half].arrived()
            w[way, s, half].start()

    w_start(0, 0)
    w_start(0, 1)

    sign = 1 - 2 * (y % 2)
    y0, y1 = y + sign, (y - sign + 4) % 4
    d0, d1 = dev(yy=y0), dev(yy=y1)
    ys = (y, y0, y1, (y + 2) % 4)
    lls = (l, 1 - l)
    rows_of = [pl.ds(k * Q, Q) for k in range(4)]

    def slot(i, s, cc=c):
        return ys[i] * 4 + lls[s] * 2 + cc

    def tcopy(src, rows, device, into):
        return Copy(t_all.at[src, rows], t_all.at[src, rows], device, t_all.at[into, rows])

    swp = [Copy(tok.at[r], t_all.at[(3 - y) * 4 + l * 2 + c, r], swap, t_all.at[t, r]) for r in rows_of]
    lx = [tcopy(slot(0, 0), r, lnb, slot(0, 1)) for r in rows_of]
    yo = {(d, s, k): tcopy(slot(0, s), rows_of[k], (d0, d1)[d], slot(1 + d, s))
          for d in range(2) for s in range(2) for k in range(4)}
    fw = {(d, s, k): tcopy(slot(2 - d, s), rows_of[k], (d0, d1)[d], slot(3, s))
          for d in range(2) for s in range(2) for k in range(4)}
    sb = {(i, s): tcopy(slot(i, s), pl.ds(0, B), sib, slot(i, s, 1 - c)) for i in range(4) for s in range(2)}
    by = {0: ((2, 3), (3,)), 1: ((0, 1, 2), (0, 1))}
    far_in = {0: ((2, 3), (0, 1)), 1: ((0, 1, 2), (3,))}

    def own(k):
        lx[k].start()
        yo[0, 0, k].start()
        yo[1, 0, k].start()

    def near_l(*ks):
        for k in ks:
            lx[k].arrived()
            yo[0, 1, k].start()
            yo[1, 1, k].start()

    def from_y(kind, d, s, ks=(0, 1, 2, 3)):
        for k in ks:
            yo[d, s, k].arrived()
            if k in by[kind][1 - d]:
                fw[1 - d, s, k].start(False)
        if 3 in ks:
            sb[1 + d, s].start()

    def far_arrived(kind, s):
        for d in range(2):
            for k in far_in[kind][d]:
                fw[d, s, k].arrived()
        sb[3, s].start()

    def fwd(yy, parts, which=None):
        yy = yy % 4

        def one(i, _):
            rr, kb = place(yy, i // 2, i % 2)

            def mm():
                for n in parts:
                    acc[n, rr] += jnp.dot(t_all[yy * 4 + i], w_all[kb, :, n * H:(n + 1) * H], preferred_element_type=F32)
            if which is None:
                mm()
            else:
                early = ((kb - z + 8 + 2) % 8) // 5
                pl.when(early == which)(mm)
            return 0
        lax.fori_loop(0, 4, one, 0)

    def place(yy, ll, cc):
        rr = (yy // 2 + h) % 2
        return rr, ((yy + rr) % 2) * 4 + ll * 2 + cc

    acc[...] = jnp.zeros_like(acc)

    def early(other):
        for i in (0, other):
            for s in range(2):
                sb[i, s].arrived()
            fwd(ys[i], (0, 1), 0)
        for s in range(2):
            sb[3 - other, s].arrived()

    @pl.when(odd == 0)
    def _():
        t_all[t] = tok[...]
        for k in range(4):
            own(k)
        sb[0, 0].start()
        w_start(1, 0)
        from_y(0, 0, 0)
        near_l(0, 1, 2, 3)
        sb[0, 1].start()
        w_start(1, 1)
        from_y(0, 1, 0, (0, 1))
        w_start(2, 0)
        from_y(0, 1, 0, (2, 3))
        w_start(2, 1)
        from_y(0, 0, 1)
        w_start(3, 0)
        from_y(0, 1, 1)
        early(1)
        far_arrived(0, 0)
        far_arrived(0, 1)

    @pl.when(odd == 1)
    def _():
        for copy in swp:
            copy.start(False)
        for k in range(4):
            swp[k].arrived()
            own(k)
            if k % 2:
                w_start(1, k // 2)
        sb[0, 0].start()
        near_l(0, 1, 2, 3)
        sb[0, 1].start()
        w_start(2, 0)
        from_y(1, 1, 0)
        from_y(1, 0, 0)
        w_start(2, 1)
        from_y(1, 1, 1)
        w_start(3, 0)
        from_y(1, 0, 1)
        early(2)
        far_arrived(1, 0)
        far_arrived(1, 1)

    w[0, 2, 1].arrived()
    w[1, 2, 0].arrived()
    w[0, 3, 0].arrived()
    w[1, 3, 1].arrived()
    fwd(y, (0, 1), 1)
    fwd((1 - odd) * y0 + odd * y1, (0, 1), 1)
    fwd(odd * y0 + (1 - odd) * y1, (0, 1))
    for s in range(2):
        sb[3, s].arrived()

    c_part, d_part = [], []
    for n in range(2):
        fwd(y + 2, (n,))

        def body(rows):
            cs[n, rows] = acc[n, 1, rows].astype(cs.dtype)
        rowwise(0, B, body)
        c_part.append(Copy(cs.at[n], cr.at[n], hpeer).start())

    for n in range(2):
        c_part[n].arrived()

        def body(rows):
            v = acc[n, 0, rows] + cr[n, rows].astype(F32)
            gate, up = v[:, :Q], v[:, Q:]
            sig = jax.nn.sigmoid(gate)
            active = gate * sig
            part = slice(n * Q, (n + 1) * Q)
            upstream = hg[rows, part].astype(F32)
            hidden_o[rows, part] = (active * up).astype(BF16)
            dg[n, 0, rows, :Q] = (upstream * up * sig * (1.0 + gate * (1.0 - sig))).astype(BF16)
            dg[n, 0, rows, Q:] = (upstream * active).astype(BF16)
        rowwise(0, B, body)
        d_part.append(Copy(dg.at[n, 0], dg.at[n, 1], hpeer).start())

    def ig_set(r, k):
        target = (odd + r + 1) % 2
        yy = (target * y0 + (1 - target) * ((y + 2) % 4)) if k == 0 else (target * y + (1 - target) * y1)

        def block(ll, cc, store):
            _, kb = place(yy, ll, cc)
            for half in range(2):
                ks = pl.ds(half * H, H)
                total = None
                for n in range(2):
                    v = lax.dot_general(dg[n, r], w_all[kb, ks, n * H:(n + 1) * H], (((1,), (1,)), ((), ())),
                                        preferred_element_type=F32)
                    total = v if total is None else total + v
                store(ll, ks, total)

        def to_other(ll, ks, v):
            igs[r, k, ll, :, ks] = v.astype(BF16)

        def to_own(ll, ks, v):
            igk[r, k, ll, :, ks] = v

        def one(ll, _):
            block(ll, 1 - c, to_other)
            return 0
        lax.fori_loop(0, 2, one, 0)
        copy = Copy(igs.at[r, k], igr.at[r, k], sib).start()

        def one(ll, _):
            block(ll, c, to_own)
            return 0
        lax.fori_loop(0, 2, one, 0)
        return copy

    def both(i, ll, rows, r):
        return igk[r, i, ll, rows] + igr[r, i, ll, rows].astype(F32)

    to_d0 = {(r, k): Copy(ds.at[r, :, rows_of[k]], dr.at[r, :, rows_of[k]], d0) for r in range(2) for k in range(4)}
    to_d1f = {k: Copy(ds.at[1 - odd, :, rows_of[k]], fr.at[:, rows_of[k]], d1) for k in (2, 3)}
    by_d1 = {0: (2, 3), 1: (3,)}
    to_d1 = [Copy(es.at[:, rows_of[k]], er.at[:, rows_of[k]], d1) for k in range(4)]
    to_l = [Copy(ls.at[rows_of[k]], lr.at[rows_of[k]], lnb) for k in range(4)]
    back = [Copy(sws.at[rows_of[k]], swr.at[rows_of[k]], swap) for k in range(4)]

    def send_d0(r, *parts, add=False):
        for k in parts:
            if add:
                to_d1f[k].arrived()
            for ll in range(2):
                def body(rows):
                    v = both(0, ll, rows, r)
                    if add:
                        v = v + fr[ll, rows].astype(F32)
                    ds[r, ll, rows] = v.astype(BF16)
                rowwise(k * Q, Q, body)
            to_d0[r, k].start(False)

    def send_merged(r, *parts):
        send_d0(r, *parts, add=True)

    def far_d1(r, *parts):
        for k in parts:
            for ll in range(2):
                def body(rows):
                    ds[r, ll, rows] = both(0, ll, rows, r).astype(BF16)
                rowwise(k * Q, Q, body)
            to_d1f[k].start(False)

    def send_d1(r, *parts):
        for k in parts:
            relay = k not in by_d1[r]
            if relay:
                to_d0[r, k].arrived()
            for ll in range(2):
                def body(rows):
                    v = both(1, ll, rows, r)
                    if relay:
                        v = v + dr[r, ll, rows].astype(F32)
                    es[ll, rows] = v.astype(BF16)
                rowwise(k * Q, Q, body)
            to_d1[k].start()

    def total(r, ll, rows):
        return both(1, ll, rows, r) + dr[r, ll, rows].astype(F32) + er[ll, rows].astype(F32)

    def send_l(r, *parts):
        for k in parts:
            to_d0[r, k].arrived()
            to_d1[k].arrived()

            def body(rows):
                ls[rows] = total(r, 1 - l, rows).astype(BF16)
            rowwise(k * Q, Q, body)
            to_l[k].start()

    def finish(r, *parts):
        for k in parts:
            to_l[k].arrived()

            def body(rows):
                v = (total(r, l, rows) + lr[rows].astype(F32)).astype(BF16)
                if r == 0:
                    ig_o[rows] = v
                else:
                    sws[rows] = v
            rowwise(k * Q, Q, body)
            if r == 1:
                back[k].start(False)

    def when(is_odd, body, *args):
        @pl.when(odd == is_odd)
        def _():
            body(*args)

    def wg_block(j, buf, n):
        j = j % 8
        for half in range(2):
            ks = pl.ds(half * H, H)
            v = None
            for rr in range(2):
                yy = 2 * ((h + rr) % 2) + (j // 4 + rr) % 2
                u = lax.dot_general(t_all[yy * 4 + j % 4, :, ks], dg[n, rr], (((0,), (0,)), ((), ())),
                                    preferred_element_type=F32)
                v = u if v is None else v + u
            wgb[buf, n, ks, :] = v

    zc = {}

    def z_step(way, s, half, n):
        add = s >= 1 if half == way else s >= 2
        if add:
            zc[way, s - 1, half, n].arrived()

        def body(rows):
            v = wgb[way, n, rows]
            if add:
                v = v + zr[way, s - 1, n, rows].astype(F32)
            zs[way, s, n, rows] = v.astype(BF16)
        rowwise(half * H, H, body)
        rows = pl.ds(half * H, H)
        zc[way, s, half, n] = Copy(zs.at[way, s, n, rows], zr.at[way, s, n, rows], right if way == 0 else left).start()

    def z_begin(n):
        wg_block(z + 4, 0, n)

        def body(rows):
            wgb[1, n, rows] = wgb[0, n, rows]
        rowwise(H, H, body)
        z_step(0, 0, 0, n)
        z_step(1, 0, 1, n)
        z_blocks(1, n)
        z_step(0, 1, 1, n)
        z_step(1, 1, 0, n)

    def z_blocks(s, n):
        wg_block(z + 4 - s, 0, n)
        wg_block(z + 4 + s, 1, n)

    def z_first(n):
        z_step(0, 1, 0, n)
        z_step(1, 1, 1, n)

    def z_next(s, n):
        z_blocks(s, n)
        z_step(0, s, 1, n)
        z_step(1, s, 0, n)
        z_step(0, s, 0, n)
        z_step(1, s, 1, n)

    a0 = ig_set(0, 0)
    d_part[0].arrived()
    z_begin(0)
    a0.arrived()
    send_d0(0, 0, 1)
    when(1, far_d1, 0, 2, 3)
    b0 = ig_set(0, 1)
    d_part[1].arrived()
    a1 = ig_set(1, 0)
    b0.arrived()
    when(1, send_d1, 0, 2, 3)
    a1.arrived()
    send_d0(1, 0, 1, 2)
    when(0, far_d1, 1, 3)
    b1 = ig_set(1, 1)
    when(1, send_d1, 0, 0, 1)
    z_begin(1)
    b1.arrived()
    when(0, send_d1, 1, 3)
    z_first(0)
    when(0, send_merged, 0, 2, 3)
    when(1, send_merged, 1, 3)
    z_first(1)
    when(0, send_d1, 1, 0)
    z_next(2, 0)

    def o_2():
        send_l(1, 1)
        finish(1, 0)

    def o_3():
        send_l(1, 2)
        finish(1, 1)

    def e_4():
        send_l(0, 1)
        finish(0, 0)
        send_l(0, 2, 3)
        finish(0, 1, 2, 3)

    def o_4():
        send_l(1, 3)
        finish(1, 2, 3)

    when(0, send_d1, 1, 1)
    when(1, send_l, 1, 0)
    z_next(2, 1)
    when(0, send_d1, 1, 2)
    when(1, o_2)
    z_next(3, 0)
    when(1, o_3)
    when(0, send_l, 0, 0)
    z_next(3, 1)
    for n in range(2):
        wg_block(z, 0, n)
    when(0, e_4)
    when(1, o_4)
    for n in range(2):
        for half in range(2):
            zc[0, 3, half, n].arrived()
            zc[1, 3, half, n].arrived()

        def body(rows):
            v = wgb[0, n, rows] + zr[0, 3, n, rows].astype(F32) + zr[1, 3, n, rows].astype(F32)
            part = slice(n * Q, (n + 1) * Q)
            gg_o[rows, part] = v[:, :Q]
            ug_o[rows, part] = v[:, Q:]
        rowwise(0, B, body)

    @pl.when(odd == 1)
    def _():
        for k in range(4):
            back[k].arrived()
            ig_o[k * Q:(k + 1) * Q] = swr[k * Q:(k + 1) * Q]
            back[k].sent()

    for copy in sends:
        copy.sent()

    def sent(kind):
        for d in range(2):
            for s in range(2):
                for k in by[kind][d]:
                    fw[d, s, k].sent()
        for r in range(2):
            for k in range(4):
                if kind == r or k not in by_d1[r]:
                    to_d0[r, k].sent()
        for k in by_d1[1 - kind]:
            to_d1f[k].sent()
        if kind == 1:
            for copy in swp:
                copy.sent()

    when(0, sent, 0)
    when(1, sent, 1)


def hand_over(*refs):
    for a, b in zip(refs[:4], refs[4:]):
        b[...] = a[...]


def body(tokens, gate_weight, up_weight, hidden_grad):
    vm = pl.BlockSpec(memory_space=pltpu.VMEM)
    results = pl.pallas_call(
        kernel,
        out_shape=(
            jax.ShapeDtypeStruct((B, H), BF16),
            jax.ShapeDtypeStruct((B, B), BF16),
            jax.ShapeDtypeStruct((B, H), F32),
            jax.ShapeDtypeStruct((B, H), F32),
        ),
        in_specs=[vm] * 4,
        out_specs=(vm,) * 4,
        scratch_shapes=[
            pltpu.VMEM((16, B, B), BF16),
            pltpu.VMEM((8, B, B), BF16),
            pltpu.VMEM((2, 2, B, H), F32),
            pltpu.VMEM((2, B, H), BF16),
            pltpu.VMEM((2, B, H), BF16),
            pltpu.VMEM((2, 2, B, H), BF16),
            pltpu.VMEM((2, 2, 2, B, B), F32),
            pltpu.VMEM((2, 2, 2, B, B), BF16),
            pltpu.VMEM((2, 2, 2, B, B), BF16),
            pltpu.VMEM((2, 2, B, B), BF16),
            pltpu.VMEM((2, 2, B, B), BF16),
            pltpu.VMEM((2, B, B), BF16),
            pltpu.VMEM((2, B, B), BF16),
            pltpu.VMEM((2, B, B), BF16),
            pltpu.VMEM((B, B), BF16),
            pltpu.VMEM((B, B), BF16),
            pltpu.VMEM((B, B), BF16),
            pltpu.VMEM((B, B), BF16),
            pltpu.VMEM((2, 2, B, H), F32),
            pltpu.VMEM((2, 4, 2, B, H), BF16),
            pltpu.VMEM((2, 4, 2, B, H), BF16),
            pltpu.SemaphoreType.DMA((N_SEMS,)),
            pltpu.SemaphoreType.DMA((N_SEMS,)),
        ],
        compiler_params=pltpu.CompilerParams(
            collective_id=0, has_side_effects=True, vmem_limit_bytes=60 * 1024 * 1024
        ),
    )(tokens, gate_weight, up_weight, hidden_grad)
    vm4 = [pl.BlockSpec(memory_space=pltpu.VMEM)] * 4
    return pl.pallas_call(
        hand_over,
        out_shape=[jax.ShapeDtypeStruct(r.shape, r.dtype) for r in results],
        in_specs=vm4,
        out_specs=vm4,
    )(*results)


def solution(mesh):
    spec = P("fsdp", "tensor")
    return jax.shard_map(body, mesh=mesh, in_specs=(spec,) * 4, out_specs=(spec,) * 4, check_vma=False)
```

```python
import functools

import jax
import jax.numpy as jnp
from jax import lax
from jax.experimental import pallas as pl
from jax.experimental.pallas import tpu as pltpu
from jax.sharding import PartitionSpec as P

MESH = pl.DeviceIdType.MESH
F32 = jnp.float32
BF16 = jnp.bfloat16
B = 512
H = 256
Q = 128
N_SEMS = 128


def kernel(tok, gw, uw, hg, hidden_o, ig_o, gg_o, ug_o,
           t_all, w_all, acc, cs, cr, dg, igk, igs, igr, ds, dr, fr, es, er, ls, lr, sws, swr, wgb, zs, zr,
           send_sem, recv_sem):
    f = lax.axis_index("fsdp")
    t = lax.axis_index("tensor")
    h, z = f // 8, f % 8
    y, l, c = t // 4, (t // 2) % 2, t % 2
    odd = (y // 2 + h) % 2

    def dev(hh=h, zz=z, yy=y, ll=l, cc=c):
        return {"tensor": (yy % 4) * 4 + ll * 2 + cc, "fsdp": hh * 8 + zz % 8}

    right, left = dev(zz=z + 1), dev(zz=z + 7)
    sib, lnb = dev(cc=1 - c), dev(ll=1 - l)
    yr, yl = dev(yy=y + 1), dev(yy=y + 3)
    swap, hpeer = dev(hh=1 - h, yy=3 - y), dev(hh=1 - h)

    barrier = pltpu.get_barrier_semaphore()
    for d in (right, left, sib, lnb, yr, yl, swap, hpeer):
        pl.semaphore_signal(barrier, inc=1, device_id=d, device_id_type=MESH)
    pl.semaphore_wait(barrier, 8)

    n_used = [0]
    sends = []

    class Copy:
        def __init__(self, src, dst, device, arrives=None):
            self.k = n_used[0]
            n_used[0] += 1
            assert self.k < N_SEMS
            self.src, self.dst, self.device = src, dst, device
            self.into = dst if arrives is None else arrives

        def make(self, src, dst):
            return pltpu.make_async_remote_copy(
                src_ref=src, dst_ref=dst, send_sem=send_sem.at[self.k], recv_sem=recv_sem.at[self.k],
                device_id=self.device, device_id_type=MESH)

        def start(self, listed=True):
            self.make(self.src, self.dst).start()
            if listed and self not in sends:
                sends.append(self)
            return self

        def arrived(self):
            self.make(self.src, self.into).wait_recv()

        def sent(self):
            self.make(self.src, self.dst).wait_send()

    def rowwise(start, size, body):
        def one(i, _):
            body(pl.ds(start + i * 64, 64))
            return 0
        lax.fori_loop(0, size // 64, one, 0)

    for n in range(2):
        part = slice(n * Q, (n + 1) * Q)
        w_all[z, :, n * H:n * H + Q] = gw[:, part]
        w_all[z, :, n * H + Q:(n + 1) * H] = uw[:, part]

    def w_copy(way, s, half):
        out, into = ((z + 8 - s) % 8, (z + 7 - s) % 8) if way == 0 else ((z + s) % 8, (z + 1 + s) % 8)
        rows = pl.ds(half * H, H)
        return Copy(w_all.at[out, rows], w_all.at[out, rows], right if way == 0 else left, w_all.at[into, rows])

    w = {}
    for s in range(4):
        for half in range(2):
            for way in range(2):
                if s < 3 or half == way:
                    w[way, s, half] = w_copy(way, s, half)

    def w_start(s, k):
        for way in range(2):
            half = way if k == 0 else 1 - way
            if s > 0:
                w[way, s - 1, half].arrived()
            w[way, s, half].start()

    w_start(0, 0)
    w_start(0, 1)

    sign = 1 - 2 * (y % 2)
    y0, y1 = y + sign, (y - sign + 4) % 4
    d0, d1 = dev(yy=y0), dev(yy=y1)
    ys = (y, y0, y1, (y + 2) % 4)
    lls = (l, 1 - l)
    rows_of = [pl.ds(k * Q, Q) for k in range(4)]

    def slot(i, s, cc=c):
        return ys[i] * 4 + lls[s] * 2 + cc

    def tcopy(src, rows, device, into):
        return Copy(t_all.at[src, rows], t_all.at[src, rows], device, t_all.at[into, rows])

    swp = [Copy(tok.at[r], t_all.at[(3 - y) * 4 + l * 2 + c, r], swap, t_all.at[t, r]) for r in rows_of]
    lx = [tcopy(slot(0, 0), r, lnb, slot(0, 1)) for r in rows_of]
    yo = {(d, s, k): tcopy(slot(0, s), rows_of[k], (d0, d1)[d], slot(1 + d, s))
          for d in range(2) for s in range(2) for k in range(4)}
    fw = {(d, s, k): tcopy(slot(2 - d, s), rows_of[k], (d0, d1)[d], slot(3, s))
          for d in range(2) for s in range(2) for k in range(4)}
    sb = {(i, s): tcopy(slot(i, s), pl.ds(0, B), sib, slot(i, s, 1 - c)) for i in range(4) for s in range(2)}
    by = {0: ((2, 3), (3,)), 1: ((0, 1, 2), (0, 1))}
    far_in = {0: ((2, 3), (0, 1)), 1: ((0, 1, 2), (3,))}

    def own(k):
        lx[k].start()
        yo[0, 0, k].start()
        yo[1, 0, k].start()

    def near_l(*ks):
        for k in ks:
            lx[k].arrived()
            yo[0, 1, k].start()
            yo[1, 1, k].start()

    def from_y(kind, d, s, ks=(0, 1, 2, 3)):
        for k in ks:
            yo[d, s, k].arrived()
            if k in by[kind][1 - d]:
                fw[1 - d, s, k].start(False)
        if 3 in ks:
            sb[1 + d, s].start()

    def far_arrived(kind, s):
        for d in range(2):
            for k in far_in[kind][d]:
                fw[d, s, k].arrived()
        sb[3, s].start()

    def fwd(yy, parts, which=None):
        yy = yy % 4

        def one(i, _):
            rr, kb = place(yy, i // 2, i % 2)

            def mm():
                for n in parts:
                    acc[n, rr] += jnp.dot(t_all[yy * 4 + i], w_all[kb, :, n * H:(n + 1) * H], preferred_element_type=F32)
            if which is None:
                mm()
            else:
                early = ((kb - z + 8 + 2) % 8) // 5
                pl.when(early == which)(mm)
            return 0
        lax.fori_loop(0, 4, one, 0)

    def place(yy, ll, cc):
        rr = (yy // 2 + h) % 2
        return rr, ((yy + rr) % 2) * 4 + ll * 2 + cc

    def early(other):
        acc[...] = jnp.zeros_like(acc)
        for i in (0, other):
            for s in range(2):
                sb[i, s].arrived()
            fwd(ys[i], (0, 1), 0)
        for s in range(2):
            sb[3 - other, s].arrived()

    @pl.when(odd == 0)
    def _():
        t_all[t] = tok[...]
        for k in range(4):
            own(k)
        sb[0, 0].start()
        w_start(1, 0)
        from_y(0, 0, 0)
        near_l(0, 1, 2, 3)
        sb[0, 1].start()
        w_start(1, 1)
        from_y(0, 1, 0, (0, 1))
        w_start(2, 0)
        from_y(0, 1, 0, (2, 3))
        w_start(2, 1)
        from_y(0, 0, 1)
        w_start(3, 0)
        from_y(0, 1, 1)
        early(1)
        far_arrived(0, 0)
        far_arrived(0, 1)

    @pl.when(odd == 1)
    def _():
        for copy in swp:
            copy.start(False)
        for k in range(4):
            swp[k].arrived()
            own(k)
            if k % 2:
                w_start(1, k // 2)
        sb[0, 0].start()
        near_l(0, 1, 2, 3)
        sb[0, 1].start()
        w_start(2, 0)
        from_y(1, 1, 0)
        from_y(1, 0, 0)
        w_start(2, 1)
        from_y(1, 1, 1)
        w_start(3, 0)
        from_y(1, 0, 1)
        early(2)
        far_arrived(1, 0)
        far_arrived(1, 1)

    w[0, 2, 1].arrived()
    w[1, 2, 0].arrived()
    w[0, 3, 0].arrived()
    w[1, 3, 1].arrived()

    c_part, d_part = [], []
    def when(is_odd, body, *args):
        @pl.when(odd == is_odd)
        def _():
            body(*args)

    def far_here():
        for s in range(2):
            sb[3, s].arrived()

    def other_even(n):
        fwd(y1, (n,))
        fwd(ys[3], (n,))

    def other_odd(n):
        fwd(y, (n,), 1)
        fwd(y0, (n,))

    def own_even():
        fwd(y, (0, 1), 1)
        fwd(y0, (0, 1), 1)

    def own_odd():
        far_here()
        fwd(y1, (0, 1), 1)
        fwd(ys[3], (0, 1))

    when(0, far_here)
    for n in range(2):
        when(0, other_even, n)
        when(1, other_odd, n)

        def body(rows):
            cs[n, rows] = acc[n, 1, rows].astype(cs.dtype)
        rowwise(0, B, body)
        c_part.append(Copy(cs.at[n], cr.at[n], hpeer).start())

    when(0, own_even)
    when(1, own_odd)
    for n in range(2):
        c_part[n].arrived()

        def body(rows):
            v = acc[n, 0, rows] + cr[n, rows].astype(F32)
            gate, up = v[:, :Q], v[:, Q:]
            sig = jax.nn.sigmoid(gate)
            active = gate * sig
            part = slice(n * Q, (n + 1) * Q)
            upstream = hg[rows, part].astype(F32)
            hidden_o[rows, part] = (active * up).astype(BF16)
            dg[n, 0, rows, :Q] = (upstream * up * sig * (1.0 + gate * (1.0 - sig))).astype(BF16)
            dg[n, 0, rows, Q:] = (upstream * active).astype(BF16)
        rowwise(0, B, body)
        d_part.append(Copy(dg.at[n, 0], dg.at[n, 1], hpeer).start())

    def ig_set(r, k):
        target = (odd + r + 1) % 2
        yy = (target * y0 + (1 - target) * ((y + 2) % 4)) if k == 0 else (target * y + (1 - target) * y1)

        def block(ll, cc, store):
            _, kb = place(yy, ll, cc)
            for half in range(2):
                ks = pl.ds(half * H, H)
                total = None
                for n in range(2):
                    v = lax.dot_general(dg[n, r], w_all[kb, ks, n * H:(n + 1) * H], (((1,), (1,)), ((), ())),
                                        preferred_element_type=F32)
                    total = v if total is None else total + v
                store(ll, ks, total)

        def to_other(ll, ks, v):
            igs[r, k, ll, :, ks] = v.astype(BF16)

        def to_own(ll, ks, v):
            igk[r, k, ll, :, ks] = v

        def one(ll, _):
            block(ll, 1 - c, to_other)
            return 0
        lax.fori_loop(0, 2, one, 0)
        copy = Copy(igs.at[r, k], igr.at[r, k], sib).start()

        def one(ll, _):
            block(ll, c, to_own)
            return 0
        lax.fori_loop(0, 2, one, 0)
        return copy

    def both(i, ll, rows, r):
        return igk[r, i, ll, rows] + igr[r, i, ll, rows].astype(F32)

    to_d0 = {(r, k): Copy(ds.at[r, :, rows_of[k]], dr.at[r, :, rows_of[k]], d0) for r in range(2) for k in range(4)}
    to_d1f = {k: Copy(ds.at[1 - odd, :, rows_of[k]], fr.at[:, rows_of[k]], d1) for k in (2, 3)}
    by_d1 = {0: (2, 3), 1: (3,)}
    to_d1 = [Copy(es.at[:, rows_of[k]], er.at[:, rows_of[k]], d1) for k in range(4)]
    to_l = [Copy(ls.at[rows_of[k]], lr.at[rows_of[k]], lnb) for k in range(4)]
    back = [Copy(sws.at[rows_of[k]], swr.at[rows_of[k]], swap) for k in range(4)]

    def send_d0(r, *parts, add=False):
        for k in parts:
            if add:
                to_d1f[k].arrived()
            for ll in range(2):
                def body(rows):
                    v = both(0, ll, rows, r)
                    if add:
                        v = v + fr[ll, rows].astype(F32)
                    ds[r, ll, rows] = v.astype(BF16)
                rowwise(k * Q, Q, body)
            to_d0[r, k].start(False)

    def send_merged(r, *parts):
        send_d0(r, *parts, add=True)

    def far_d1(r, *parts):
        for k in parts:
            for ll in range(2):
                def body(rows):
                    ds[r, ll, rows] = both(0, ll, rows, r).astype(BF16)
                rowwise(k * Q, Q, body)
            to_d1f[k].start(False)

    def send_d1(r, *parts):
        for k in parts:
            relay = k not in by_d1[r]
            if relay:
                to_d0[r, k].arrived()
            for ll in range(2):
                def body(rows):
                    v = both(1, ll, rows, r)
                    if relay:
                        v = v + dr[r, ll, rows].astype(F32)
                    es[ll, rows] = v.astype(BF16)
                rowwise(k * Q, Q, body)
            to_d1[k].start()

    def total(r, ll, rows):
        return both(1, ll, rows, r) + dr[r, ll, rows].astype(F32) + er[ll, rows].astype(F32)

    def send_l(r, *parts):
        for k in parts:
            to_d0[r, k].arrived()
            to_d1[k].arrived()

            def body(rows):
                ls[rows] = total(r, 1 - l, rows).astype(BF16)
            rowwise(k * Q, Q, body)
            to_l[k].start()

    def finish(r, *parts):
        for k in parts:
            to_l[k].arrived()

            def body(rows):
                v = (total(r, l, rows) + lr[rows].astype(F32)).astype(BF16)
                if r == 0:
                    ig_o[rows] = v
                else:
                    sws[rows] = v
            rowwise(k * Q, Q, body)
            if r == 1:
                back[k].start(False)

    def wg_block(j, buf, n):
        j = j % 8
        for half in range(2):
            ks = pl.ds(half * H, H)
            v = None
            for rr in range(2):
                yy = 2 * ((h + rr) % 2) + (j // 4 + rr) % 2
                u = lax.dot_general(t_all[yy * 4 + j % 4, :, ks], dg[n, rr], (((0,), (0,)), ((), ())),
                                    preferred_element_type=F32)
                v = u if v is None else v + u
            wgb[buf, n, ks, :] = v

    zc = {}

    def z_step(way, s, half, n):
        add = s >= 1 if half == way else s >= 2
        if add:
            zc[way, s - 1, half, n].arrived()

        def body(rows):
            v = wgb[way, n, rows]
            if add:
                v = v + zr[way, s - 1, n, rows].astype(F32)
            zs[way, s, n, rows] = v.astype(BF16)
        rowwise(half * H, H, body)
        rows = pl.ds(half * H, H)
        zc[way, s, half, n] = Copy(zs.at[way, s, n, rows], zr.at[way, s, n, rows], right if way == 0 else left).start()

    def z_begin(n):
        wg_block(z + 4, 0, n)

        def body(rows):
            wgb[1, n, rows] = wgb[0, n, rows]
        rowwise(H, H, body)
        z_step(0, 0, 0, n)
        z_step(1, 0, 1, n)
        z_blocks(1, n)
        z_step(0, 1, 1, n)
        z_step(1, 1, 0, n)

    def z_blocks(s, n):
        wg_block(z + 4 - s, 0, n)
        wg_block(z + 4 + s, 1, n)

    def z_first(n):
        z_step(0, 1, 0, n)
        z_step(1, 1, 1, n)

    def z_next(s, n):
        z_blocks(s, n)
        z_step(0, s, 1, n)
        z_step(1, s, 0, n)
        z_step(0, s, 0, n)
        z_step(1, s, 1, n)

    a0 = ig_set(0, 0)
    d_part[0].arrived()
    z_begin(0)
    a0.arrived()
    send_d0(0, 0, 1)
    when(1, far_d1, 0, 2, 3)
    b0 = ig_set(0, 1)
    d_part[1].arrived()
    a1 = ig_set(1, 0)
    b0.arrived()
    when(1, send_d1, 0, 2, 3)
    a1.arrived()
    send_d0(1, 0, 1, 2)
    when(0, far_d1, 1, 3)
    b1 = ig_set(1, 1)
    when(1, send_d1, 0, 0, 1)
    z_begin(1)
    b1.arrived()
    when(0, send_d1, 1, 3)
    z_first(0)
    when(0, send_merged, 0, 2, 3)
    when(1, send_merged, 1, 3)
    z_first(1)
    when(0, send_d1, 1, 0)
    z_next(2, 0)

    def o_2():
        send_l(1, 1)
        finish(1, 0)

    def o_3():
        send_l(1, 2)
        finish(1, 1)

    def e_4():
        send_l(0, 1)
        finish(0, 0)
        send_l(0, 2, 3)
        finish(0, 1, 2, 3)

    def o_4():
        send_l(1, 3)
        finish(1, 2, 3)

    when(0, send_d1, 1, 1)
    when(1, send_l, 1, 0)
    z_next(2, 1)
    when(0, send_d1, 1, 2)
    when(1, o_2)
    z_next(3, 0)
    when(1, o_3)
    when(0, send_l, 0, 0)
    z_next(3, 1)
    for n in range(2):
        wg_block(z, 0, n)
    when(0, e_4)
    when(1, o_4)
    for n in range(2):
        for half in range(2):
            zc[0, 3, half, n].arrived()
            zc[1, 3, half, n].arrived()

        def body(rows):
            v = wgb[0, n, rows] + zr[0, 3, n, rows].astype(F32) + zr[1, 3, n, rows].astype(F32)
            part = slice(n * Q, (n + 1) * Q)
            gg_o[rows, part] = v[:, :Q]
            ug_o[rows, part] = v[:, Q:]
        rowwise(0, B, body)

    @pl.when(odd == 1)
    def _():
        for k in range(4):
            back[k].arrived()
            ig_o[k * Q:(k + 1) * Q] = swr[k * Q:(k + 1) * Q]
            back[k].sent()

    for copy in sends:
        copy.sent()

    def sent(kind):
        for d in range(2):
            for s in range(2):
                for k in by[kind][d]:
                    fw[d, s, k].sent()
        for r in range(2):
            for k in range(4):
                if kind == r or k not in by_d1[r]:
                    to_d0[r, k].sent()
        for k in by_d1[1 - kind]:
            to_d1f[k].sent()
        if kind == 1:
            for copy in swp:
                copy.sent()

    when(0, sent, 0)
    when(1, sent, 1)


def hand_over(*refs):
    for a, b in zip(refs[:4], refs[4:]):
        b[...] = a[...]


def body(tokens, gate_weight, up_weight, hidden_grad):
    vm = pl.BlockSpec(memory_space=pltpu.VMEM)
    results = pl.pallas_call(
        kernel,
        out_shape=(
            jax.ShapeDtypeStruct((B, H), BF16),
            jax.ShapeDtypeStruct((B, B), BF16),
            jax.ShapeDtypeStruct((B, H), F32),
            jax.ShapeDtypeStruct((B, H), F32),
        ),
        in_specs=[vm] * 4,
        out_specs=(vm,) * 4,
        scratch_shapes=[
            pltpu.VMEM((16, B, B), BF16),
            pltpu.VMEM((8, B, B), BF16),
            pltpu.VMEM((2, 2, B, H), F32),
            pltpu.VMEM((2, B, H), BF16),
            pltpu.VMEM((2, B, H), BF16),
            pltpu.VMEM((2, 2, B, H), BF16),
            pltpu.VMEM((2, 2, 2, B, B), F32),
            pltpu.VMEM((2, 2, 2, B, B), BF16),
            pltpu.VMEM((2, 2, 2, B, B), BF16),
            pltpu.VMEM((2, 2, B, B), BF16),
            pltpu.VMEM((2, 2, B, B), BF16),
            pltpu.VMEM((2, B, B), BF16),
            pltpu.VMEM((2, B, B), BF16),
            pltpu.VMEM((2, B, B), BF16),
            pltpu.VMEM((B, B), BF16),
            pltpu.VMEM((B, B), BF16),
            pltpu.VMEM((B, B), BF16),
            pltpu.VMEM((B, B), BF16),
            pltpu.VMEM((2, 2, B, H), F32),
            pltpu.VMEM((2, 4, 2, B, H), BF16),
            pltpu.VMEM((2, 4, 2, B, H), BF16),
            pltpu.SemaphoreType.DMA((N_SEMS,)),
            pltpu.SemaphoreType.DMA((N_SEMS,)),
        ],
        compiler_params=pltpu.CompilerParams(
            collective_id=0, has_side_effects=True, vmem_limit_bytes=60 * 1024 * 1024
        ),
    )(tokens, gate_weight, up_weight, hidden_grad)
    vm4 = [pl.BlockSpec(memory_space=pltpu.VMEM)] * 4
    return pl.pallas_call(
        hand_over,
        out_shape=[jax.ShapeDtypeStruct(r.shape, r.dtype) for r in results],
        in_specs=vm4,
        out_specs=vm4,
    )(*results)


def solution(mesh):
    spec = P("fsdp", "tensor")
    return jax.shard_map(body, mesh=mesh, in_specs=(spec,) * 4, out_specs=(spec,) * 4, check_vma=False)
```

```python
import functools

import jax
import jax.numpy as jnp
from jax import lax
from jax.experimental import pallas as pl
from jax.experimental.pallas import tpu as pltpu
from jax.sharding import PartitionSpec as P

MESH = pl.DeviceIdType.MESH
F32 = jnp.float32
BF16 = jnp.bfloat16
B = 512
H = 256
Q = 128
N_SEMS = 128


def kernel(tok, gw, uw, hg, hidden_o, ig_o, gg_o, ug_o,
           t_all, w_all, acc, cs, cr, dg, igk, igs, igr, ds, dr, fr, es, er, ls, lr, sws, swr, wgb, zs, zr,
           send_sem, recv_sem):
    f = lax.axis_index("fsdp")
    t = lax.axis_index("tensor")
    h, z = f // 8, f % 8
    y, l, c = t // 4, (t // 2) % 2, t % 2
    odd = (y // 2 + h) % 2

    def dev(hh=h, zz=z, yy=y, ll=l, cc=c):
        return {"tensor": (yy % 4) * 4 + ll * 2 + cc, "fsdp": hh * 8 + zz % 8}

    right, left = dev(zz=z + 1), dev(zz=z + 7)
    sib, lnb = dev(cc=1 - c), dev(ll=1 - l)
    yr, yl = dev(yy=y + 1), dev(yy=y + 3)
    swap, hpeer = dev(hh=1 - h, yy=3 - y), dev(hh=1 - h)

    barrier = pltpu.get_barrier_semaphore()
    for d in (right, left, sib, lnb, yr, yl, swap, hpeer):
        pl.semaphore_signal(barrier, inc=1, device_id=d, device_id_type=MESH)
    pl.semaphore_wait(barrier, 8)

    n_used = [0]
    sends = []

    class Copy:
        def __init__(self, src, dst, device, arrives=None):
            self.k = n_used[0]
            n_used[0] += 1
            assert self.k < N_SEMS
            self.src, self.dst, self.device = src, dst, device
            self.into = dst if arrives is None else arrives

        def make(self, src, dst):
            return pltpu.make_async_remote_copy(
                src_ref=src, dst_ref=dst, send_sem=send_sem.at[self.k], recv_sem=recv_sem.at[self.k],
                device_id=self.device, device_id_type=MESH)

        def start(self, listed=True):
            self.make(self.src, self.dst).start()
            if listed and self not in sends:
                sends.append(self)
            return self

        def arrived(self):
            self.make(self.src, self.into).wait_recv()

        def sent(self):
            self.make(self.src, self.dst).wait_send()

    def rowwise(start, size, body):
        def one(i, _):
            body(pl.ds(start + i * 64, 64))
            return 0
        lax.fori_loop(0, size // 64, one, 0)

    for n in range(2):
        part = slice(n * Q, (n + 1) * Q)
        w_all[z, :, n * H:n * H + Q] = gw[:, part]
        w_all[z, :, n * H + Q:(n + 1) * H] = uw[:, part]

    def w_copy(way, s, half):
        out, into = ((z + 8 - s) % 8, (z + 7 - s) % 8) if way == 0 else ((z + s) % 8, (z + 1 + s) % 8)
        rows = pl.ds(half * H, H)
        return Copy(w_all.at[out, rows], w_all.at[out, rows], right if way == 0 else left, w_all.at[into, rows])

    w = {}
    for s in range(4):
        for half in range(2):
            for way in range(2):
                if s < 3 or half == way:
                    w[way, s, half] = w_copy(way, s, half)

    def w_start(s, k):
        for way in range(2):
            half = way if k == 0 else 1 - way
            if s > 0:
                w[way, s - 1, half].arrived()
            w[way, s, half].start()

    w_start(0, 0)
    w_start(0, 1)

    sign = 1 - 2 * (y % 2)
    y0, y1 = y + sign, (y - sign + 4) % 4
    d0, d1 = dev(yy=y0), dev(yy=y1)
    ys = (y, y0, y1, (y + 2) % 4)
    lls = (l, 1 - l)
    rows_of = [pl.ds(k * Q, Q) for k in range(4)]

    def slot(i, s, cc=c):
        return ys[i] * 4 + lls[s] * 2 + cc

    def tcopy(src, rows, device, into):
        return Copy(t_all.at[src, rows], t_all.at[src, rows], device, t_all.at[into, rows])

    swp = [Copy(tok.at[r], t_all.at[(3 - y) * 4 + l * 2 + c, r], swap, t_all.at[t, r]) for r in rows_of]
    lx = [tcopy(slot(0, 0), r, lnb, slot(0, 1)) for r in rows_of]
    yo = {(d, s, k): tcopy(slot(0, s), rows_of[k], (d0, d1)[d], slot(1 + d, s))
          for d in range(2) for s in range(2) for k in range(4)}
    fw = {(d, s, k): tcopy(slot(2 - d, s), rows_of[k], (d0, d1)[d], slot(3, s))
          for d in range(2) for s in range(2) for k in range(4)}
    sb = {(i, s): tcopy(slot(i, s), pl.ds(0, B), sib, slot(i, s, 1 - c)) for i in range(4) for s in range(2)}
    by = {0: ((2, 3), (3,)), 1: ((0, 1, 2), (0, 1))}
    far_in = {0: ((2, 3), (0, 1)), 1: ((0, 1, 2), (3,))}

    def own(k):
        lx[k].start()
        yo[0, 0, k].start()
        yo[1, 0, k].start()

    def near_l(*ks):
        for k in ks:
            lx[k].arrived()
            yo[0, 1, k].start()
            yo[1, 1, k].start()

    def from_y(kind, d, s, ks=(0, 1, 2, 3)):
        for k in ks:
            yo[d, s, k].arrived()
            if k in by[kind][1 - d]:
                fw[1 - d, s, k].start(False)
        if 3 in ks:
            sb[1 + d, s].start()

    def far_arrived(kind, s):
        for d in range(2):
            for k in far_in[kind][d]:
                fw[d, s, k].arrived()
        sb[3, s].start()

    def fwd(yy, parts, which=None):
        yy = yy % 4

        def one(i, _):
            rr, kb = place(yy, i // 2, i % 2)

            def mm():
                for n in parts:
                    acc[n, rr] += jnp.dot(t_all[yy * 4 + i], w_all[kb, :, n * H:(n + 1) * H], preferred_element_type=F32)
            if which is None:
                mm()
            else:
                early = ((kb - z + 8 + 2) % 8) // 5
                pl.when(early == which)(mm)
            return 0
        lax.fori_loop(0, 4, one, 0)

    def place(yy, ll, cc):
        rr = (yy // 2 + h) % 2
        return rr, ((yy + rr) % 2) * 4 + ll * 2 + cc

    def early(other):
        acc[...] = jnp.zeros_like(acc)
        for i in (0, other):
            for s in range(2):
                sb[i, s].arrived()
            fwd(ys[i], (0, 1), 0)
        for s in range(2):
            sb[3 - other, s].arrived()

    @pl.when(odd == 0)
    def _():
        t_all[t] = tok[...]
        for k in range(4):
            own(k)
        sb[0, 0].start()
        w_start(1, 0)
        from_y(0, 0, 0)
        near_l(0, 1, 2, 3)
        sb[0, 1].start()
        w_start(1, 1)
        from_y(0, 1, 0, (0, 1))
        w_start(2, 0)
        from_y(0, 1, 0, (2, 3))
        w_start(2, 1)
        from_y(0, 0, 1)
        w_start(3, 0)
        from_y(0, 1, 1)
        early(1)
        far_arrived(0, 0)
        far_arrived(0, 1)

    @pl.when(odd == 1)
    def _():
        for copy in swp:
            copy.start(False)
        for k in range(4):
            swp[k].arrived()
            own(k)
            if k % 2:
                w_start(1, k // 2)
        sb[0, 0].start()
        near_l(0, 1, 2, 3)
        sb[0, 1].start()
        w_start(2, 0)
        from_y(1, 1, 0)
        from_y(1, 0, 0)
        w_start(2, 1)
        from_y(1, 1, 1)
        w_start(3, 0)
        from_y(1, 0, 1)
        early(2)
        far_arrived(1, 0)
        far_arrived(1, 1)

    w[0, 2, 1].arrived()
    w[1, 2, 0].arrived()
    w[0, 3, 0].arrived()
    w[1, 3, 1].arrived()

    c_part, d_part = [], []
    def when(is_odd, body, *args):
        @pl.when(odd == is_odd)
        def _():
            body(*args)

    def far_here():
        for s in range(2):
            sb[3, s].arrived()

    def other_even(n):
        fwd(y1, (n,))
        fwd(ys[3], (n,))

    def other_odd(n):
        fwd(y, (n,), 1)
        fwd(y0, (n,))

    def own_even():
        fwd(y, (0, 1), 1)
        fwd(y0, (0, 1), 1)

    def own_odd():
        far_here()
        fwd(y1, (0, 1), 1)
        fwd(ys[3], (0, 1))

    when(0, far_here)
    for n in range(2):
        when(0, other_even, n)
        when(1, other_odd, n)

        def body(rows):
            cs[n, rows] = acc[n, 1, rows].astype(cs.dtype)
        rowwise(0, B, body)
        c_part.append(Copy(cs.at[n], cr.at[n], hpeer).start())

    when(0, own_even)
    when(1, own_odd)
    for n in range(2):
        c_part[n].arrived()

        def body(rows):
            v = acc[n, 0, rows] + cr[n, rows].astype(F32)
            gate, up = v[:, :Q], v[:, Q:]
            sig = jax.nn.sigmoid(gate)
            active = gate * sig
            part = slice(n * Q, (n + 1) * Q)
            upstream = hg[rows, part].astype(F32)
            hidden_o[rows, part] = (active * up).astype(BF16)
            dg[n, 0, rows, :Q] = (upstream * up * sig * (1.0 + gate * (1.0 - sig))).astype(BF16)
            dg[n, 0, rows, Q:] = (upstream * active).astype(BF16)
        rowwise(0, B, body)
        d_part.append(Copy(dg.at[n, 0], dg.at[n, 1], hpeer).start())

    def ig_set(r, k):
        target = (odd + r + 1) % 2
        yy = (target * y0 + (1 - target) * ((y + 2) % 4)) if k == 0 else (target * y + (1 - target) * y1)

        def block(ll, cc, store):
            _, kb = place(yy, ll, cc)
            for half in range(2):
                ks = pl.ds(half * H, H)
                total = None
                for n in range(2):
                    v = lax.dot_general(dg[n, r], w_all[kb, ks, n * H:(n + 1) * H], (((1,), (1,)), ((), ())),
                                        preferred_element_type=F32)
                    total = v if total is None else total + v
                store(ll, ks, total)

        def to_other(ll, ks, v):
            igs[r, k, ll, :, ks] = v.astype(BF16)

        def to_own(ll, ks, v):
            igk[r, k, ll, :, ks] = v

        def one(ll, _):
            block(ll, 1 - c, to_other)
            return 0
        lax.fori_loop(0, 2, one, 0)
        copy = Copy(igs.at[r, k], igr.at[r, k], sib).start()

        def one(ll, _):
            block(ll, c, to_own)
            return 0
        lax.fori_loop(0, 2, one, 0)
        return copy

    def both(i, ll, rows, r):
        return igk[r, i, ll, rows] + igr[r, i, ll, rows].astype(F32)

    to_d0 = {(r, k): Copy(ds.at[r, :, rows_of[k]], dr.at[r, :, rows_of[k]], d0) for r in range(2) for k in range(4)}
    to_d1f = {k: Copy(ds.at[1 - odd, :, rows_of[k]], fr.at[:, rows_of[k]], d1) for k in (2, 3)}
    by_d1 = {0: (2, 3), 1: (3,)}
    to_d1 = [Copy(es.at[:, rows_of[k]], er.at[:, rows_of[k]], d1) for k in range(4)]
    to_l = [Copy(ls.at[rows_of[k]], lr.at[rows_of[k]], lnb) for k in range(4)]
    back = [Copy(sws.at[rows_of[k]], swr.at[rows_of[k]], swap) for k in range(4)]

    def send_d0(r, *parts, add=False):
        for k in parts:
            if add:
                to_d1f[k].arrived()
            for ll in range(2):
                def body(rows):
                    v = both(0, ll, rows, r)
                    if add:
                        v = v + fr[ll, rows].astype(F32)
                    ds[r, ll, rows] = v.astype(BF16)
                rowwise(k * Q, Q, body)
            to_d0[r, k].start(False)

    def send_merged(r, *parts):
        send_d0(r, *parts, add=True)

    def far_d1(r, *parts):
        for k in parts:
            for ll in range(2):
                def body(rows):
                    ds[r, ll, rows] = both(0, ll, rows, r).astype(BF16)
                rowwise(k * Q, Q, body)
            to_d1f[k].start(False)

    def send_d1(r, *parts):
        for k in parts:
            relay = k not in by_d1[r]
            if relay:
                to_d0[r, k].arrived()
            for ll in range(2):
                def body(rows):
                    v = both(1, ll, rows, r)
                    if relay:
                        v = v + dr[r, ll, rows].astype(F32)
                    es[ll, rows] = v.astype(BF16)
                rowwise(k * Q, Q, body)
            to_d1[k].start()

    def total(r, ll, rows):
        return both(1, ll, rows, r) + dr[r, ll, rows].astype(F32) + er[ll, rows].astype(F32)

    def send_l(r, *parts):
        for k in parts:
            to_d0[r, k].arrived()
            to_d1[k].arrived()

            def body(rows):
                ls[rows] = total(r, 1 - l, rows).astype(BF16)
            rowwise(k * Q, Q, body)
            to_l[k].start()

    def finish(r, *parts):
        for k in parts:
            to_l[k].arrived()

            def body(rows):
                v = (total(r, l, rows) + lr[rows].astype(F32)).astype(BF16)
                if r == 0:
                    ig_o[rows] = v
                else:
                    sws[rows] = v
            rowwise(k * Q, Q, body)
            if r == 1:
                back[k].start(False)

    def wg_block(j, buf, n):
        j = j % 8
        for half in range(2):
            ks = pl.ds(half * H, H)
            v = None
            for rr in range(2):
                yy = 2 * ((h + rr) % 2) + (j // 4 + rr) % 2
                u = lax.dot_general(t_all[yy * 4 + j % 4, :, ks], dg[n, rr], (((0,), (0,)), ((), ())),
                                    preferred_element_type=F32)
                v = u if v is None else v + u
            wgb[buf, n, ks, :] = v

    zc = {}

    def z_step(way, s, half, n):
        add = s >= 1 if half == way else s >= 2
        if add:
            zc[way, s - 1, half, n].arrived()

        def body(rows):
            v = wgb[way, n, rows]
            if add:
                v = v + zr[way, s - 1, n, rows].astype(F32)
            zs[way, s, n, rows] = v.astype(BF16)
        rowwise(half * H, H, body)
        rows = pl.ds(half * H, H)
        zc[way, s, half, n] = Copy(zs.at[way, s, n, rows], zr.at[way, s, n, rows], right if way == 0 else left).start()

    def z_begin(n):
        wg_block(z + 4, 0, n)

        def body(rows):
            wgb[1, n, rows] = wgb[0, n, rows]
        rowwise(H, H, body)
        z_step(0, 0, 0, n)
        z_step(1, 0, 1, n)
        z_blocks(1, n)
        z_step(0, 1, 1, n)
        z_step(1, 1, 0, n)

    def z_blocks(s, n):
        wg_block(z + 4 - s, 0, n)
        wg_block(z + 4 + s, 1, n)

    def z_first(n):
        z_step(0, 1, 0, n)
        z_step(1, 1, 1, n)

    def z_next(s, n):
        z_blocks(s, n)
        z_step(0, s, 1, n)
        z_step(1, s, 0, n)
        z_step(0, s, 0, n)
        z_step(1, s, 1, n)

    a0 = ig_set(0, 0)
    d_part[0].arrived()
    z_begin(0)
    a0.arrived()
    send_d0(0, 0, 1)
    when(1, far_d1, 0, 2, 3)
    b0 = ig_set(0, 1)
    d_part[1].arrived()
    a1 = ig_set(1, 0)
    z_begin(1)
    b0.arrived()
    when(1, send_d1, 0, 2, 3)
    a1.arrived()
    send_d0(1, 0, 1, 2)
    when(0, far_d1, 1, 3)
    b1 = ig_set(1, 1)
    when(1, send_d1, 0, 0, 1)
    b1.arrived()
    when(0, send_d1, 1, 3)
    z_first(0)
    when(0, send_merged, 0, 2, 3)
    when(1, send_merged, 1, 3)
    z_first(1)
    when(0, send_d1, 1, 0)
    z_next(2, 0)

    def o_2():
        send_l(1, 1)
        finish(1, 0)

    def o_3():
        send_l(1, 2)
        finish(1, 1)

    def e_4():
        send_l(0, 1)
        finish(0, 0)
        send_l(0, 2, 3)
        finish(0, 1, 2, 3)

    def o_4():
        send_l(1, 3)
        finish(1, 2, 3)

    when(0, send_d1, 1, 1)
    when(1, send_l, 1, 0)
    z_next(2, 1)
    when(0, send_d1, 1, 2)
    when(1, o_2)
    z_next(3, 0)
    when(1, o_3)
    when(0, send_l, 0, 0)
    z_next(3, 1)
    for n in range(2):
        wg_block(z, 0, n)
    when(0, e_4)
    when(1, o_4)
    for n in range(2):
        for half in range(2):
            zc[0, 3, half, n].arrived()
            zc[1, 3, half, n].arrived()

        def body(rows):
            v = wgb[0, n, rows] + zr[0, 3, n, rows].astype(F32) + zr[1, 3, n, rows].astype(F32)
            part = slice(n * Q, (n + 1) * Q)
            gg_o[rows, part] = v[:, :Q]
            ug_o[rows, part] = v[:, Q:]
        rowwise(0, B, body)

    @pl.when(odd == 1)
    def _():
        for k in range(4):
            back[k].arrived()
            ig_o[k * Q:(k + 1) * Q] = swr[k * Q:(k + 1) * Q]
            back[k].sent()

    for copy in sends:
        copy.sent()

    def sent(kind):
        for d in range(2):
            for s in range(2):
                for k in by[kind][d]:
                    fw[d, s, k].sent()
        for r in range(2):
            for k in range(4):
                if kind == r or k not in by_d1[r]:
                    to_d0[r, k].sent()
        for k in by_d1[1 - kind]:
            to_d1f[k].sent()
        if kind == 1:
            for copy in swp:
                copy.sent()

    when(0, sent, 0)
    when(1, sent, 1)


def hand_over(*refs):
    for a, b in zip(refs[:4], refs[4:]):
        b[...] = a[...]


def body(tokens, gate_weight, up_weight, hidden_grad):
    vm = pl.BlockSpec(memory_space=pltpu.VMEM)
    results = pl.pallas_call(
        kernel,
        out_shape=(
            jax.ShapeDtypeStruct((B, H), BF16),
            jax.ShapeDtypeStruct((B, B), BF16),
            jax.ShapeDtypeStruct((B, H), F32),
            jax.ShapeDtypeStruct((B, H), F32),
        ),
        in_specs=[vm] * 4,
        out_specs=(vm,) * 4,
        scratch_shapes=[
            pltpu.VMEM((16, B, B), BF16),
            pltpu.VMEM((8, B, B), BF16),
            pltpu.VMEM((2, 2, B, H), F32),
            pltpu.VMEM((2, B, H), BF16),
            pltpu.VMEM((2, B, H), BF16),
            pltpu.VMEM((2, 2, B, H), BF16),
            pltpu.VMEM((2, 2, 2, B, B), F32),
            pltpu.VMEM((2, 2, 2, B, B), BF16),
            pltpu.VMEM((2, 2, 2, B, B), BF16),
            pltpu.VMEM((2, 2, B, B), BF16),
            pltpu.VMEM((2, 2, B, B), BF16),
            pltpu.VMEM((2, B, B), BF16),
            pltpu.VMEM((2, B, B), BF16),
            pltpu.VMEM((2, B, B), BF16),
            pltpu.VMEM((B, B), BF16),
            pltpu.VMEM((B, B), BF16),
            pltpu.VMEM((B, B), BF16),
            pltpu.VMEM((B, B), BF16),
            pltpu.VMEM((2, 2, B, H), F32),
            pltpu.VMEM((2, 4, 2, B, H), BF16),
            pltpu.VMEM((2, 4, 2, B, H), BF16),
            pltpu.SemaphoreType.DMA((N_SEMS,)),
            pltpu.SemaphoreType.DMA((N_SEMS,)),
        ],
        compiler_params=pltpu.CompilerParams(
            collective_id=0, has_side_effects=True, vmem_limit_bytes=60 * 1024 * 1024
        ),
    )(tokens, gate_weight, up_weight, hidden_grad)
    vm4 = [pl.BlockSpec(memory_space=pltpu.VMEM)] * 4
    return pl.pallas_call(
        hand_over,
        out_shape=[jax.ShapeDtypeStruct(r.shape, r.dtype) for r in results],
        in_specs=vm4,
        out_specs=vm4,
    )(*results)


def solution(mesh):
    spec = P("fsdp", "tensor")
    return jax.shard_map(body, mesh=mesh, in_specs=(spec,) * 4, out_specs=(spec,) * 4, check_vma=False)
```

```python
import functools

import jax
import jax.numpy as jnp
from jax import lax
from jax.experimental import pallas as pl
from jax.experimental.pallas import tpu as pltpu
from jax.sharding import PartitionSpec as P

MESH = pl.DeviceIdType.MESH
F32 = jnp.float32
BF16 = jnp.bfloat16
B = 512
H = 256
Q = 128
N_SEMS = 128


def kernel(tok, gw, uw, hg, hidden_o, ig_o, gg_o, ug_o,
           t_all, w_all, acc, cs, cr, dg, igk, igs, igr, ds, dr, fr, es, er, ls, lr, sws, swr, wgb, zs, zr,
           send_sem, recv_sem):
    f = lax.axis_index("fsdp")
    t = lax.axis_index("tensor")
    h, z = f // 8, f % 8
    y, l, c = t // 4, (t // 2) % 2, t % 2
    odd = (y // 2 + h) % 2

    def dev(hh=h, zz=z, yy=y, ll=l, cc=c):
        return {"tensor": (yy % 4) * 4 + ll * 2 + cc, "fsdp": hh * 8 + zz % 8}

    right, left = dev(zz=z + 1), dev(zz=z + 7)
    sib, lnb = dev(cc=1 - c), dev(ll=1 - l)
    yr, yl = dev(yy=y + 1), dev(yy=y + 3)
    swap, hpeer = dev(hh=1 - h, yy=3 - y), dev(hh=1 - h)

    barrier = pltpu.get_barrier_semaphore()
    for d in (right, left, sib, lnb, yr, yl, swap, hpeer):
        pl.semaphore_signal(barrier, inc=1, device_id=d, device_id_type=MESH)
    for n in range(2):
        part = slice(n * Q, (n + 1) * Q)
        w_all[z, :, n * H:n * H + Q] = gw[:, part]
        w_all[z, :, n * H + Q:(n + 1) * H] = uw[:, part]

    @pl.when(odd == 0)
    def _():
        t_all[t] = tok[...]

    pl.semaphore_wait(barrier, 8)

    n_used = [0]
    sends = []

    class Copy:
        def __init__(self, src, dst, device, arrives=None):
            self.k = n_used[0]
            n_used[0] += 1
            assert self.k < N_SEMS
            self.src, self.dst, self.device = src, dst, device
            self.into = dst if arrives is None else arrives

        def make(self, src, dst):
            return pltpu.make_async_remote_copy(
                src_ref=src, dst_ref=dst, send_sem=send_sem.at[self.k], recv_sem=recv_sem.at[self.k],
                device_id=self.device, device_id_type=MESH)

        def start(self, listed=True):
            self.make(self.src, self.dst).start()
            if listed and self not in sends:
                sends.append(self)
            return self

        def arrived(self):
            self.make(self.src, self.into).wait_recv()

        def sent(self):
            self.make(self.src, self.dst).wait_send()

    def rowwise(start, size, body):
        def one(i, _):
            body(pl.ds(start + i * 64, 64))
            return 0
        lax.fori_loop(0, size // 64, one, 0)

    def w_copy(way, s, half):
        out, into = ((z + 8 - s) % 8, (z + 7 - s) % 8) if way == 0 else ((z + s) % 8, (z + 1 + s) % 8)
        rows = pl.ds(half * H, H)
        return Copy(w_all.at[out, rows], w_all.at[out, rows], right if way == 0 else left, w_all.at[into, rows])

    w = {}
    for s in range(4):
        for half in range(2):
            for way in range(2):
                if s < 3 or half == way:
                    w[way, s, half] = w_copy(way, s, half)

    def w_start(s, k):
        for way in range(2):
            half = way if k == 0 else 1 - way
            if s > 0:
                w[way, s - 1, half].arrived()
            w[way, s, half].start()

    w_start(0, 0)
    w_start(0, 1)

    sign = 1 - 2 * (y % 2)
    y0, y1 = y + sign, (y - sign + 4) % 4
    d0, d1 = dev(yy=y0), dev(yy=y1)
    ys = (y, y0, y1, (y + 2) % 4)
    lls = (l, 1 - l)
    rows_of = [pl.ds(k * Q, Q) for k in range(4)]

    def slot(i, s, cc=c):
        return ys[i] * 4 + lls[s] * 2 + cc

    def tcopy(src, rows, device, into):
        return Copy(t_all.at[src, rows], t_all.at[src, rows], device, t_all.at[into, rows])

    swp = [Copy(tok.at[r], t_all.at[(3 - y) * 4 + l * 2 + c, r], swap, t_all.at[t, r]) for r in rows_of]
    lx = [tcopy(slot(0, 0), r, lnb, slot(0, 1)) for r in rows_of]
    yo = {(d, s, k): tcopy(slot(0, s), rows_of[k], (d0, d1)[d], slot(1 + d, s))
          for d in range(2) for s in range(2) for k in range(4)}
    fw = {(d, s, k): tcopy(slot(2 - d, s), rows_of[k], (d0, d1)[d], slot(3, s))
          for d in range(2) for s in range(2) for k in range(4)}
    sb = {(i, s): tcopy(slot(i, s), pl.ds(0, B), sib, slot(i, s, 1 - c)) for i in range(4) for s in range(2)}
    by = {0: ((2, 3), (3,)), 1: ((0, 1, 2), (0, 1))}
    far_in = {0: ((2, 3), (0, 1)), 1: ((0, 1, 2), (3,))}

    def own(k):
        lx[k].start()
        yo[0, 0, k].start()
        yo[1, 0, k].start()

    def near_l(*ks):
        for k in ks:
            lx[k].arrived()
            yo[0, 1, k].start()
            yo[1, 1, k].start()

    def from_y(kind, d, s, ks=(0, 1, 2, 3)):
        for k in ks:
            yo[d, s, k].arrived()
            if k in by[kind][1 - d]:
                fw[1 - d, s, k].start(False)
        if 3 in ks:
            sb[1 + d, s].start()

    def far_arrived(kind, s):
        for d in range(2):
            for k in far_in[kind][d]:
                fw[d, s, k].arrived()
        sb[3, s].start()

    def fwd(yy, parts, which=None):
        yy = yy % 4

        def one(i, _):
            rr, kb = place(yy, i // 2, i % 2)

            def mm():
                for n in parts:
                    acc[n, rr] += jnp.dot(t_all[yy * 4 + i], w_all[kb, :, n * H:(n + 1) * H], preferred_element_type=F32)
            if which is None:
                mm()
            else:
                early = ((kb - z + 8 + 2) % 8) // 5
                pl.when(early == which)(mm)
            return 0
        lax.fori_loop(0, 4, one, 0)

    def place(yy, ll, cc):
        rr = (yy // 2 + h) % 2
        return rr, ((yy + rr) % 2) * 4 + ll * 2 + cc

    def early(other):
        acc[...] = jnp.zeros_like(acc)
        for i in (0, other):
            for s in range(2):
                sb[i, s].arrived()
            fwd(ys[i], (0, 1), 0)
        for s in range(2):
            sb[3 - other, s].arrived()

    @pl.when(odd == 0)
    def _():
        for k in range(4):
            own(k)
        sb[0, 0].start()
        w_start(1, 0)
        from_y(0, 0, 0)
        near_l(0, 1, 2, 3)
        sb[0, 1].start()
        w_start(1, 1)
        from_y(0, 1, 0, (0, 1))
        w_start(2, 0)
        from_y(0, 1, 0, (2, 3))
        w_start(2, 1)
        from_y(0, 0, 1)
        w_start(3, 0)
        from_y(0, 1, 1)
        early(1)
        far_arrived(0, 0)
        far_arrived(0, 1)

    @pl.when(odd == 1)
    def _():
        for copy in swp:
            copy.start(False)
        for k in range(4):
            swp[k].arrived()
            own(k)
            if k % 2:
                w_start(1, k // 2)
        sb[0, 0].start()
        near_l(0, 1, 2, 3)
        sb[0, 1].start()
        w_start(2, 0)
        from_y(1, 1, 0)
        from_y(1, 0, 0)
        w_start(2, 1)
        from_y(1, 1, 1)
        w_start(3, 0)
        from_y(1, 0, 1)
        early(2)
        far_arrived(1, 0)
        far_arrived(1, 1)

    w[0, 2, 1].arrived()
    w[1, 2, 0].arrived()
    w[0, 3, 0].arrived()
    w[1, 3, 1].arrived()

    c_part, d_part = [], []
    def when(is_odd, body, *args):
        @pl.when(odd == is_odd)
        def _():
            body(*args)

    def far_here():
        for s in range(2):
            sb[3, s].arrived()

    def other_even(n):
        fwd(y1, (n,))
        fwd(ys[3], (n,))

    def other_odd(n):
        fwd(y, (n,), 1)
        fwd(y0, (n,))

    def own_even():
        fwd(y, (0, 1), 1)
        fwd(y0, (0, 1), 1)

    def own_odd():
        far_here()
        fwd(y1, (0, 1), 1)
        fwd(ys[3], (0, 1))

    when(0, far_here)
    for n in range(2):
        when(0, other_even, n)
        when(1, other_odd, n)

        def body(rows):
            cs[n, rows] = acc[n, 1, rows].astype(cs.dtype)
        rowwise(0, B, body)
        c_part.append(Copy(cs.at[n], cr.at[n], hpeer).start())

    when(0, own_even)
    when(1, own_odd)
    for n in range(2):
        c_part[n].arrived()

        def body(rows):
            v = acc[n, 0, rows] + cr[n, rows].astype(F32)
            gate, up = v[:, :Q], v[:, Q:]
            sig = jax.nn.sigmoid(gate)
            active = gate * sig
            part = slice(n * Q, (n + 1) * Q)
            upstream = hg[rows, part].astype(F32)
            hidden_o[rows, part] = (active * up).astype(BF16)
            dg[n, 0, rows, :Q] = (upstream * up * sig * (1.0 + gate * (1.0 - sig))).astype(BF16)
            dg[n, 0, rows, Q:] = (upstream * active).astype(BF16)
        rowwise(0, B, body)
        d_part.append(Copy(dg.at[n, 0], dg.at[n, 1], hpeer).start())

    def ig_set(r, k):
        target = (odd + r + 1) % 2
        yy = (target * y0 + (1 - target) * ((y + 2) % 4)) if k == 0 else (target * y + (1 - target) * y1)

        def block(ll, cc, store):
            _, kb = place(yy, ll, cc)
            for half in range(2):
                ks = pl.ds(half * H, H)
                total = None
                for n in range(2):
                    v = lax.dot_general(dg[n, r], w_all[kb, ks, n * H:(n + 1) * H], (((1,), (1,)), ((), ())),
                                        preferred_element_type=F32)
                    total = v if total is None else total + v
                store(ll, ks, total)

        def to_other(ll, ks, v):
            igs[r, k, ll, :, ks] = v.astype(BF16)

        def to_own(ll, ks, v):
            igk[r, k, ll, :, ks] = v

        def one(ll, _):
            block(ll, 1 - c, to_other)
            return 0
        lax.fori_loop(0, 2, one, 0)
        copy = Copy(igs.at[r, k], igr.at[r, k], sib).start()

        def one(ll, _):
            block(ll, c, to_own)
            return 0
        lax.fori_loop(0, 2, one, 0)
        return copy

    def both(i, ll, rows, r):
        return igk[r, i, ll, rows] + igr[r, i, ll, rows].astype(F32)

    to_d0 = {(r, k): Copy(ds.at[r, :, rows_of[k]], dr.at[r, :, rows_of[k]], d0) for r in range(2) for k in range(4)}
    to_d1f = {k: Copy(ds.at[1 - odd, :, rows_of[k]], fr.at[:, rows_of[k]], d1) for k in (2, 3)}
    by_d1 = {0: (2, 3), 1: (3,)}
    to_d1 = [Copy(es.at[:, rows_of[k]], er.at[:, rows_of[k]], d1) for k in range(4)]
    to_l = [Copy(ls.at[rows_of[k]], lr.at[rows_of[k]], lnb) for k in range(4)]
    back = [Copy(sws.at[rows_of[k]], swr.at[rows_of[k]], swap) for k in range(4)]

    def send_d0(r, *parts, add=False):
        for k in parts:
            if add:
                to_d1f[k].arrived()
            for ll in range(2):
                def body(rows):
                    v = both(0, ll, rows, r)
                    if add:
                        v = v + fr[ll, rows].astype(F32)
                    ds[r, ll, rows] = v.astype(BF16)
                rowwise(k * Q, Q, body)
            to_d0[r, k].start(False)

    def send_merged(r, *parts):
        send_d0(r, *parts, add=True)

    def far_d1(r, *parts):
        for k in parts:
            for ll in range(2):
                def body(rows):
                    ds[r, ll, rows] = both(0, ll, rows, r).astype(BF16)
                rowwise(k * Q, Q, body)
            to_d1f[k].start(False)

    def send_d1(r, *parts):
        for k in parts:
            relay = k not in by_d1[r]
            if relay:
                to_d0[r, k].arrived()
            for ll in range(2):
                def body(rows):
                    v = both(1, ll, rows, r)
                    if relay:
                        v = v + dr[r, ll, rows].astype(F32)
                    es[ll, rows] = v.astype(BF16)
                rowwise(k * Q, Q, body)
            to_d1[k].start()

    def total(r, ll, rows):
        return both(1, ll, rows, r) + dr[r, ll, rows].astype(F32) + er[ll, rows].astype(F32)

    def send_l(r, *parts):
        for k in parts:
            to_d0[r, k].arrived()
            to_d1[k].arrived()

            def body(rows):
                ls[rows] = total(r, 1 - l, rows).astype(BF16)
            rowwise(k * Q, Q, body)
            to_l[k].start()

    def finish(r, *parts):
        for k in parts:
            to_l[k].arrived()

            def body(rows):
                v = (total(r, l, rows) + lr[rows].astype(F32)).astype(BF16)
                if r == 0:
                    ig_o[rows] = v
                else:
                    sws[rows] = v
            rowwise(k * Q, Q, body)
            if r == 1:
                back[k].start(False)

    def wg_block(j, buf, n):
        j = j % 8
        for half in range(2):
            ks = pl.ds(half * H, H)
            v = None
            for rr in range(2):
                yy = 2 * ((h + rr) % 2) + (j // 4 + rr) % 2
                u = lax.dot_general(t_all[yy * 4 + j % 4, :, ks], dg[n, rr], (((0,), (0,)), ((), ())),
                                    preferred_element_type=F32)
                v = u if v is None else v + u
            wgb[buf, n, ks, :] = v

    zc = {}

    def z_step(way, s, half, n):
        add = s >= 1 if half == way else s >= 2
        if add:
            zc[way, s - 1, half, n].arrived()

        def body(rows):
            v = wgb[way, n, rows]
            if add:
                v = v + zr[way, s - 1, n, rows].astype(F32)
            zs[way, s, n, rows] = v.astype(BF16)
        rowwise(half * H, H, body)
        rows = pl.ds(half * H, H)
        zc[way, s, half, n] = Copy(zs.at[way, s, n, rows], zr.at[way, s, n, rows], right if way == 0 else left).start()

    def z_begin(n):
        wg_block(z + 4, 0, n)

        def body(rows):
            wgb[1, n, rows] = wgb[0, n, rows]
        rowwise(H, H, body)
        z_step(0, 0, 0, n)
        z_step(1, 0, 1, n)
        z_blocks(1, n)
        z_step(0, 1, 1, n)
        z_step(1, 1, 0, n)

    def z_blocks(s, n):
        wg_block(z + 4 - s, 0, n)
        wg_block(z + 4 + s, 1, n)

    def z_first(n):
        z_step(0, 1, 0, n)
        z_step(1, 1, 1, n)

    def z_next(s, n):
        z_blocks(s, n)
        z_step(0, s, 1, n)
        z_step(1, s, 0, n)
        z_step(0, s, 0, n)
        z_step(1, s, 1, n)

    a0 = ig_set(0, 0)
    d_part[0].arrived()
    z_begin(0)
    a0.arrived()
    send_d0(0, 0, 1)
    when(1, far_d1, 0, 2, 3)
    b0 = ig_set(0, 1)
    d_part[1].arrived()
    a1 = ig_set(1, 0)
    b0.arrived()
    when(1, send_d1, 0, 2, 3)
    a1.arrived()
    send_d0(1, 0, 1, 2)
    when(0, far_d1, 1, 3)
    b1 = ig_set(1, 1)
    when(1, send_d1, 0, 0, 1)
    z_begin(1)
    b1.arrived()
    when(0, send_d1, 1, 3)
    z_first(0)
    when(0, send_merged, 0, 2, 3)
    when(1, send_merged, 1, 3)
    z_first(1)
    when(0, send_d1, 1, 0)
    z_next(2, 0)

    def o_2():
        send_l(1, 1)
        finish(1, 0)

    def o_3():
        send_l(1, 2)
        finish(1, 1)

    def e_4():
        send_l(0, 1)
        finish(0, 0)
        send_l(0, 2, 3)
        finish(0, 1, 2, 3)

    def o_4():
        send_l(1, 3)
        finish(1, 2, 3)

    when(0, send_d1, 1, 1)
    when(1, send_l, 1, 0)
    z_next(2, 1)
    when(0, send_d1, 1, 2)
    when(1, o_2)
    z_next(3, 0)
    when(1, o_3)
    when(0, send_l, 0, 0)
    z_next(3, 1)
    for n in range(2):
        wg_block(z, 0, n)
    when(0, e_4)
    when(1, o_4)
    for n in range(2):
        for half in range(2):
            zc[0, 3, half, n].arrived()
            zc[1, 3, half, n].arrived()

        def body(rows):
            v = wgb[0, n, rows] + zr[0, 3, n, rows].astype(F32) + zr[1, 3, n, rows].astype(F32)
            part = slice(n * Q, (n + 1) * Q)
            gg_o[rows, part] = v[:, :Q]
            ug_o[rows, part] = v[:, Q:]
        rowwise(0, B, body)

    @pl.when(odd == 1)
    def _():
        for k in range(4):
            back[k].arrived()
            ig_o[k * Q:(k + 1) * Q] = swr[k * Q:(k + 1) * Q]
            back[k].sent()

    for copy in sends:
        copy.sent()

    def sent(kind):
        for d in range(2):
            for s in range(2):
                for k in by[kind][d]:
                    fw[d, s, k].sent()
        for r in range(2):
            for k in range(4):
                if kind == r or k not in by_d1[r]:
                    to_d0[r, k].sent()
        for k in by_d1[1 - kind]:
            to_d1f[k].sent()
        if kind == 1:
            for copy in swp:
                copy.sent()

    when(0, sent, 0)
    when(1, sent, 1)


def hand_over(*refs):
    for a, b in zip(refs[:4], refs[4:]):
        b[...] = a[...]


def body(tokens, gate_weight, up_weight, hidden_grad):
    vm = pl.BlockSpec(memory_space=pltpu.VMEM)
    results = pl.pallas_call(
        kernel,
        out_shape=(
            jax.ShapeDtypeStruct((B, H), BF16),
            jax.ShapeDtypeStruct((B, B), BF16),
            jax.ShapeDtypeStruct((B, H), F32),
            jax.ShapeDtypeStruct((B, H), F32),
        ),
        in_specs=[vm] * 4,
        out_specs=(vm,) * 4,
        scratch_shapes=[
            pltpu.VMEM((16, B, B), BF16),
            pltpu.VMEM((8, B, B), BF16),
            pltpu.VMEM((2, 2, B, H), F32),
            pltpu.VMEM((2, B, H), BF16),
            pltpu.VMEM((2, B, H), BF16),
            pltpu.VMEM((2, 2, B, H), BF16),
            pltpu.VMEM((2, 2, 2, B, B), F32),
            pltpu.VMEM((2, 2, 2, B, B), BF16),
            pltpu.VMEM((2, 2, 2, B, B), BF16),
            pltpu.VMEM((2, 2, B, B), BF16),
            pltpu.VMEM((2, 2, B, B), BF16),
            pltpu.VMEM((2, B, B), BF16),
            pltpu.VMEM((2, B, B), BF16),
            pltpu.VMEM((2, B, B), BF16),
            pltpu.VMEM((B, B), BF16),
            pltpu.VMEM((B, B), BF16),
            pltpu.VMEM((B, B), BF16),
            pltpu.VMEM((B, B), BF16),
            pltpu.VMEM((2, 2, B, H), F32),
            pltpu.VMEM((2, 4, 2, B, H), BF16),
            pltpu.VMEM((2, 4, 2, B, H), BF16),
            pltpu.SemaphoreType.DMA((N_SEMS,)),
            pltpu.SemaphoreType.DMA((N_SEMS,)),
        ],
        compiler_params=pltpu.CompilerParams(
            collective_id=0, has_side_effects=True, vmem_limit_bytes=60 * 1024 * 1024
        ),
    )(tokens, gate_weight, up_weight, hidden_grad)
    vm4 = [pl.BlockSpec(memory_space=pltpu.VMEM)] * 4
    return pl.pallas_call(
        hand_over,
        out_shape=[jax.ShapeDtypeStruct(r.shape, r.dtype) for r in results],
        in_specs=vm4,
        out_specs=vm4,
    )(*results)


def solution(mesh):
    spec = P("fsdp", "tensor")
    return jax.shard_map(body, mesh=mesh, in_specs=(spec,) * 4, out_specs=(spec,) * 4, check_vma=False)
```
